32 devices in a mesh: row: 4 (over y, core), col: 8 (over z, x).
Axes of the slice: x: 2, y: 2, z: 4, core: 2. Of those that a mesh axis runs over, the one named last changes fastest.
Arguments:
- rhs_low: bfloat16 [8192, 512], P(('row', 'col')), may hold values from -6 to 6
- rhs_top: bfloat16 [4096, 512], P('row'), may hold values from -6 to 6
- lower_blocks: bfloat16 [64, 64, 128, 128], P('row', 'col'), may hold values from -0.046875 to 0.046875
- upper_blocks: bfloat16 [64, 64, 128, 128], P('row', 'col'), may hold values from -0.0625 to 0.0625
- block_target: int32 [64, 64], P('row', 'col'), may hold values from 0 to 7
- inv_lower_low: bfloat16 [64, 128, 128], P(('row', 'col')), as said below
- inv_upper_low: bfloat16 [64, 128, 128], P(('row', 'col')), as said below
- inv_lower_top: bfloat16 [32, 128, 128], P('row'), as said below
- inv_upper_top: bfloat16 [32, 128, 128], P('row'), as said below
Outputs:
- sol_low: bfloat16 [8192, 512], P(('row', 'col'))
- sol_top: bfloat16 [4096, 512], P(('row', 'col'))
The draws below stay inside these ranges and needn't reach their ends.
Inputs may be any that keep to these rules, and one draw needn't show every extreme that they name: `inv_lower_low`: lower triangular with nonzero diagonal. `inv_upper_low`: upper triangular with nonzero diagonal. `inv_lower_top`: lower triangular with nonzero diagonal. `inv_upper_top`: upper triangular with nonzero diagonal.
All inputs are finite; a program needn't handle non-finite values.
Results may differ from the reference program's by a relative error of at most 0.024.
Values may be sent and summed in bfloat16 or wider, within the bound.
No kernel may reach another device: no remote copies, remote signals or barrier semaphores. Data moves between devices by JAX's collectives and lax.ppermute only.
A program may use at most 128 MiB of HBM per device.

```python
import math
import jax
import jax.numpy as jnp
from jax import lax

B = 128
NRHS = 512
E = 16
K1R = 2
P2D = 1
N1 = 64
P2 = 8
N2 = 32
EROWS = 64
N_ROW = 4
N_COL = 8


def triangular(key, count, lower):
    values = jax.random.normal(key, (count, B, B), jnp.float32) * (1.5 / math.sqrt(B))
    scales = jax.random.uniform(jax.random.fold_in(key, 7), (count, B, B), jnp.float32, 0.5, 2.0)
    rows = lax.broadcasted_iota(jnp.int32, (B, B), 0)
    cols = lax.broadcasted_iota(jnp.int32, (B, B), 1)
    if lower:
        keep = rows > cols
    else:
        keep = rows < cols
    return jnp.where(keep[None], values, jnp.where((rows == cols)[None], scales, 0.0))


def draw_inv_lower_low(key, part):
    return triangular(jax.random.fold_in(key, 11), N1, True).astype(jnp.bfloat16)


def draw_inv_upper_low(key, part):
    return triangular(jax.random.fold_in(key, 12), N1, False).astype(jnp.bfloat16)


def draw_inv_lower_top(key, part):
    return triangular(jax.random.fold_in(key, 13), N2, True).astype(jnp.bfloat16)


def draw_inv_upper_top(key, part):
    return triangular(jax.random.fold_in(key, 14), N2, False).astype(jnp.bfloat16)


def touch_ends(drawn, rng, low, top_value):
    spot = [jax.random.randint(jax.random.fold_in(rng, axis), (), 0, length) for axis, length in enumerate(drawn.shape)]
    main_axis = drawn.shape.index(max(drawn.shape))
    next_to = spot[:main_axis] + [(spot[main_axis] + 1) % drawn.shape[main_axis]] + spot[main_axis + 1:]
    return drawn.at[tuple(spot)].set(low).at[tuple(next_to)].set(top_value)


def shard_levels(key, dims, shards, smallest, high):
    level, own = 1.0, jax.random.fold_in(key, 6)
    for dim, shards_of in shards:
        steps = jnp.exp(jax.random.uniform(jax.random.fold_in(own, dim), (shards_of,), jnp.float32, smallest / len(shards), high / len(shards)))
        level = level * jnp.repeat(steps, dims[dim] // shards_of).reshape([-1 if axis == dim else 1 for axis in range(len(dims))])
    return level


def gaussian(own_key, dims, deviation, limit, cuts=(), kind=jnp.bfloat16):
    values = deviation * jax.random.normal(own_key, dims, jnp.float32)
    if cuts:
        values = values * shard_levels(own_key, dims, cuts, -0.22, 0.18)
    return jnp.clip(values, -limit, limit).astype(kind)


def setup_inputs(seed: int = 0) -> dict:
    key_list = jax.random.split(jax.random.key(seed), 10)
    return {
        "rhs_low": gaussian(key_list[0], (N1 * B, NRHS), 1.0, 6.0, ((0, 32),)),
        "rhs_top": gaussian(key_list[1], (N2 * B, NRHS), 1.0, 6.0, ((0, 4),)),
        "lower_blocks": gaussian(key_list[2], (EROWS, N1, B, B), (B * E * K1R * N_ROW // P2D) ** -0.5, 0.046875, ((0, 4), (1, 8))),
        "upper_blocks": gaussian(key_list[3], (EROWS, N1, B, B), (B * E * N_ROW) ** -0.5, 0.0625, ((0, 4), (1, 8))),
        "block_target": touch_ends(jax.random.randint(key_list[4], (EROWS, N1), 0, P2), jax.random.fold_in(key_list[4], 1), 0, P2 - 1).astype(jnp.int32),
        "inv_lower_low": draw_inv_lower_low(jax.random.fold_in(key_list[9], 71), 0),
        "inv_upper_low": draw_inv_upper_low(jax.random.fold_in(key_list[9], 71), 0),
        "inv_lower_top": draw_inv_lower_top(jax.random.fold_in(key_list[9], 71), 0),
        "inv_upper_top": draw_inv_upper_top(jax.random.fold_in(key_list[9], 71), 0),
    }


def forward_partial(row, col, fwd_grid, lower_blocks, block_target):
    column = lax.dynamic_index_in_dim(fwd_grid, col, 1, keepdims=False).reshape(N_ROW * K1R, B, NRHS)
    blocks = lax.dynamic_slice_in_dim(lax.dynamic_slice_in_dim(lower_blocks, row * E, E, 0), col * (N_ROW * K1R), N_ROW * K1R, 1)
    targets = lax.dynamic_slice_in_dim(lax.dynamic_slice_in_dim(block_target, row * E, E, 0), col * (N_ROW * K1R), N_ROW * K1R, 1)
    slots = jnp.arange(P2D * N_COL, dtype=jnp.int32)
    column_f = column.astype(jnp.float32)

    def step(total, item):
        blk, tgt = item
        prod = jnp.einsum('kab,kbj->kaj', blk.astype(jnp.float32), column_f)
        onehot = (tgt[:, None] == slots[None, :]).astype(jnp.float32)
        return total + jnp.einsum('kp,kaj->paj', onehot, prod, precision=lax.Precision.HIGHEST), None

    start = jnp.zeros((P2D * N_COL, B, NRHS), jnp.float32)
    total, _ = lax.scan(step, start, (blocks, targets))
    return total.astype(jnp.bfloat16)


def backward_partial(row, col, top_grid, upper_blocks, block_target):
    solved = lax.dynamic_index_in_dim(top_grid, row, 0, keepdims=False)
    blocks = lax.dynamic_slice_in_dim(lax.dynamic_slice_in_dim(upper_blocks, row * E, E, 0), col * (N_ROW * K1R), N_ROW * K1R, 1)
    targets = lax.dynamic_slice_in_dim(lax.dynamic_slice_in_dim(block_target, row * E, E, 0), col * (N_ROW * K1R), N_ROW * K1R, 1)

    def step(total, item):
        blk, tgt = item
        picked = jnp.take(solved, tgt, axis=0).astype(jnp.float32)
        return total + jnp.einsum('kab,kbj->kaj', blk.astype(jnp.float32), picked), None

    start = jnp.zeros((N_ROW * K1R, B, NRHS), jnp.float32)
    total, _ = lax.scan(step, start, (blocks, targets))
    return total.astype(jnp.bfloat16)


def reference(rhs_low, rhs_top, lower_blocks, upper_blocks, block_target, inv_lower_low, inv_upper_low, inv_lower_top, inv_upper_top):
    count_low = K1R * N_ROW * N_COL
    count_top = P2D * N_COL * N_ROW
    rhs_blocks = rhs_low.reshape(count_low, B, NRHS).astype(jnp.float32)
    fwd_low = jnp.einsum('kab,kbj->kaj', inv_lower_low.astype(jnp.float32), rhs_blocks).astype(jnp.bfloat16)
    fwd_grid = fwd_low.reshape(N_ROW, N_COL, K1R, B, NRHS)
    rows = jnp.arange(N_ROW, dtype=jnp.int32)
    cols = jnp.arange(N_COL, dtype=jnp.int32)

    def row_sum(row):
        parts = lax.map(lambda col: forward_partial(row, col, fwd_grid, lower_blocks, block_target), cols)
        return jnp.sum(parts.astype(jnp.float32), axis=0)

    lsum = lax.map(row_sum, rows).reshape(count_top, B, NRHS)
    resid_top = (rhs_top.reshape(count_top, B, NRHS).astype(jnp.float32) - lsum).astype(jnp.bfloat16)
    fwd_top = jnp.einsum('kab,kbj->kaj', inv_lower_top.astype(jnp.float32), resid_top.astype(jnp.float32)).astype(jnp.bfloat16)
    sol_top = jnp.einsum('kab,kbj->kaj', inv_upper_top.astype(jnp.float32), fwd_top.astype(jnp.float32)).astype(jnp.bfloat16)
    top_grid = sol_top.reshape(N_ROW, P2D * N_COL, B, NRHS)

    def col_sum(col):
        parts = lax.map(lambda row: backward_partial(row, col, top_grid, upper_blocks, block_target), rows)
        return jnp.sum(parts.astype(jnp.float32), axis=0)

    usum = lax.map(col_sum, cols).reshape(N_COL, N_ROW, K1R, B, NRHS)
    usum = jnp.transpose(usum, (1, 0, 2, 3, 4)).reshape(count_low, B, NRHS)
    resid_low = (fwd_low.astype(jnp.float32) - usum).astype(jnp.bfloat16)
    sol_low = jnp.einsum('kab,kbj->kaj', inv_upper_low.astype(jnp.float32), resid_low.astype(jnp.float32)).astype(jnp.bfloat16)
    return sol_low.reshape(count_low * B, NRHS), sol_top.reshape(count_top * B, NRHS)
```

```python
import functools

import jax
import jax.numpy as jnp
from jax import lax
from jax.experimental import pallas as pl
from jax.experimental.pallas import tpu as pltpu
from jax.sharding import PartitionSpec as P

BF = jnp.bfloat16
F32 = jnp.float32
CHUNKS = 1
SLOT = {3: 0, 1: 1, 2: 2, 0: 3}
ORDER = (3, 1, 2, 0)
MIB = 1 << 20


def params(mib, **kw):
    return pltpu.CompilerParams(vmem_limit_bytes=mib * MIB, **kw)


def place_of(rel, count):
    low = rel & 3
    slot = jnp.where(low == 0, 3, jnp.where(low == 3, 0, low))
    return slot * (count // 4) + (rel >> 2)


def fwd_kernel(inv_ref, rhs_ref, *outs):
    own, width, _ = inv_ref.shape
    per = rhs_ref.shape[1] // len(outs)
    for j in range(own):
        rows = slice(j * width, (j + 1) * width)
        for i, out in enumerate(outs):
            out[rows, :] = jnp.dot(
                inv_ref[j], rhs_ref[rows, i * per : (i + 1) * per], preferred_element_type=F32
            ).astype(BF)


def solve_fwd(inv, rhs, chunks):
    rows, cols = rhs.shape
    return pl.pallas_call(
        fwd_kernel,
        out_shape=[jax.ShapeDtypeStruct((rows, cols // chunks), BF)] * chunks,
        compiler_params=params(8),
        name="fwd_low",
    )(inv, rhs)


def sum_kernel(lower, rows, tops, own, steps, ids_ref, tgt_ref, blk_ref, out_ref, acc_ref):
    step = pl.program_id(0)
    per, count, width, _ = blk_ref.shape
    me_row, me_col = ids_ref[0], ids_ref[1]

    @pl.when(step == 0)
    def _():
        acc_ref[...] = jnp.zeros(acc_ref.shape, F32)

    for e in range(per):
        for m in range(count):
            rel_top = tgt_ref[m, step * per + e] ^ me_col
            rel_row = (m // own) ^ me_row
            blk = blk_ref[e, m].astype(F32)
            if lower:
                at = pl.multiple_of(place_of(rel_top, tops) * width, width)
                lanes = slice((m % own) * width, (m % own + 1) * width)
                acc_ref[rel_row, pl.ds(at, width), lanes] += blk
            else:
                at = pl.multiple_of((place_of(rel_row, rows) * own + m % own) * width, width)
                acc_ref[rel_top, pl.ds(at, width), :] += blk

    @pl.when(step == steps - 1)
    def _():
        for i in range(out_ref.shape[0]):
            out_ref[i] = acc_ref[i].astype(BF)


def sum_blocks(lower, ids, targets, blocks, rows, tops, own):
    slots, count, width, _ = blocks.shape
    steps = 4
    shape = (rows, tops * width, own * width) if lower else (tops, rows * own * width, width)
    return pl.pallas_call(
        functools.partial(sum_kernel, lower, rows, tops, own, steps),
        grid_spec=pltpu.PrefetchScalarGridSpec(
            num_scalar_prefetch=2,
            grid=(steps,),
            in_specs=[
                pl.BlockSpec((slots // steps, count, width, width), lambda i, a, b: (i, 0, 0, 0)),
            ],
            out_specs=pl.BlockSpec(shape, lambda i, a, b: (0, 0, 0)),
            scratch_shapes=[pltpu.VMEM(shape, F32)],
        ),
        out_shape=jax.ShapeDtypeStruct(shape, BF),
        compiler_params=params(40),
        name="sum_lower" if lower else "sum_upper",
        cost_estimate=pl.CostEstimate(flops=4 * blocks.size, bytes_accessed=3 * blocks.size, transcendentals=0),
    )(ids, targets, blocks)


def lower_kernel(mat_ref, p0, p1, p2, p3, *outs):
    pieces = (p0, p1, p2, p3)
    per = outs[0].shape[0]
    deep = mat_ref.shape[2]
    for i, out in enumerate(outs):
        total = None
        for s in range(mat_ref.shape[0]):
            part = jnp.dot(
                mat_ref[s, i * per : (i + 1) * per, :],
                pieces[s % 4][(s // 4) * deep : (s // 4 + 1) * deep, :],
                preferred_element_type=F32,
            )
            total = part if total is None else total + part
        out[...] = total.astype(BF)


def apply_lower(mat, pieces):
    rows, cols = mat.shape[1], pieces[0].shape[1]
    return pl.pallas_call(
        lower_kernel,
        out_shape=[jax.ShapeDtypeStruct((rows // 4, cols), BF)] * 4,
        compiler_params=params(32),
        name="apply_lower",
        cost_estimate=pl.CostEstimate(
            flops=2 * mat.size * cols, bytes_accessed=2 * mat.size + 4 * rows * cols, transcendentals=0
        ),
    )(mat, *pieces)


def upper_kernel(mat_ref, p0, p1, p2, p3, first, two, zero):
    pieces = (p0, p1, p2, p3)
    rows = mat_ref.shape[1]
    per = rows // 4
    groups = mat_ref.shape[0] // 4
    for i in range(4):
        total = None
        for g in range(4):
            left = jnp.concatenate(
                [mat_ref[g + 4 * h, i * per : (i + 1) * per, :] for h in range(groups)], axis=1
            )
            part = jnp.dot(left, pieces[g][...], preferred_element_type=F32)
            total = part if total is None else total + part
        total = total.astype(BF)
        if i < 2:
            first[i * per : (i + 1) * per, :] = total
        elif i == 2:
            two[...] = total
        else:
            zero[...] = total


def apply_upper(mat, pieces):
    rows, cols = mat.shape[1], pieces[0].shape[1]
    return pl.pallas_call(
        upper_kernel,
        out_shape=[
            jax.ShapeDtypeStruct((rows // 2, cols), BF),
            jax.ShapeDtypeStruct((rows // 4, cols), BF),
            jax.ShapeDtypeStruct((rows // 4, cols), BF),
        ],
        compiler_params=params(32),
        name="apply_upper",
        cost_estimate=pl.CostEstimate(
            flops=2 * mat.size * cols, bytes_accessed=2 * mat.size + 4 * rows * cols, transcendentals=0
        ),
    )(mat, *pieces)


def top_kernel(parts, own, aliased, ids_ref, rhs_ref, low_ref, up_ref, *refs):
    terms, out, copy = refs[:parts], refs[-2], refs[-1]
    width = low_ref.shape[1]
    for k in range(own):
        rows = slice(k * width, (k + 1) * width)
        lsum = terms[0][rows, :].astype(F32)
        for term in terms[1:]:
            lsum = lsum + term[rows, :].astype(F32)
        resid = (rhs_ref[rows, :].astype(F32) - lsum).astype(BF)
        fwd = jnp.dot(low_ref[k], resid, preferred_element_type=F32).astype(BF)
        sol = jnp.dot(up_ref[k], fwd, preferred_element_type=F32).astype(BF)
        out[rows, :] = sol
        copy[rows, :] = sol


def solve_top(ids, rhs_top, inv_low, inv_up, terms, into, chunk, chunks):
    tops, width, _ = inv_low.shape
    own, cols = terms[0].shape[0] // width, terms[0].shape[1]
    whole = jax.ShapeDtypeStruct((own * width, cols * chunks), BF)
    more = [] if into is None else [into]
    return pl.pallas_call(
        functools.partial(top_kernel, len(terms), own, bool(more)),
        grid_spec=pltpu.PrefetchScalarGridSpec(
            num_scalar_prefetch=1,
            grid=(1,),
            in_specs=[
                pl.BlockSpec((own * width, cols), lambda i, a: (a[1], chunk)),
                pl.BlockSpec((own, width, width), lambda i, a: (a[1], 0, 0)),
                pl.BlockSpec((own, width, width), lambda i, a: (a[1], 0, 0)),
            ]
            + [pl.BlockSpec((own * width, cols), lambda i, a: (0, 0))] * len(terms)
            + [pl.BlockSpec(memory_space=pl.ANY)] * len(more),
            out_specs=[
                pl.BlockSpec((own * width, cols), lambda i, a: (0, chunk)),
                pl.BlockSpec((own * width, cols), lambda i, a: (0, 0)),
            ],
        ),
        out_shape=[whole, jax.ShapeDtypeStruct((own * width, cols), BF)],
        input_output_aliases={4 + len(terms): 0} if more else {},
        compiler_params=params(8),
        name="solve_top",
    )(ids, rhs_top, inv_low, inv_up, *terms, *more)


def low_kernel(parts, inv_ref, fwd_ref, *refs):
    terms, out = refs[:parts], refs[-1]
    own, width, _ = inv_ref.shape
    for j in range(own):
        rows = slice(j * width, (j + 1) * width)
        usum = terms[0][rows, :].astype(F32)
        for term in terms[1:]:
            usum = usum + term[rows, :].astype(F32)
        resid = (fwd_ref[rows, :].astype(F32) - usum).astype(BF)
        out[rows, :] = jnp.dot(inv_ref[j], resid, preferred_element_type=F32).astype(BF)


def solve_low(inv, fwd, terms, into, chunk, chunks):
    rows, cols = fwd.shape
    more = [] if into is None else [into]
    return pl.pallas_call(
        functools.partial(low_kernel, len(terms)),
        grid=(1,),
        in_specs=[
            pl.BlockSpec(inv.shape, lambda i: (0, 0, 0)),
            pl.BlockSpec((rows, cols), lambda i: (0, 0)),
        ]
        + [pl.BlockSpec((rows, cols), lambda i, at=at: (at, 0)) for _, at in terms]
        + [pl.BlockSpec(memory_space=pl.ANY)] * len(more),
        out_specs=pl.BlockSpec((rows, cols), lambda i: (0, chunk)),
        out_shape=jax.ShapeDtypeStruct((rows, cols * chunks), BF),
        input_output_aliases={2 + len(terms): 0} if more else {},
        compiler_params=params(8),
        name="solve_low",
    )(inv, fwd, *[t for t, _ in terms], *more)


def swap(x, axis, bit):
    size = lax.axis_size(axis)
    return lax.ppermute(x, axis, [(i, i ^ (1 << bit)) for i in range(size)])


def add(*xs):
    total = xs[0].astype(F32)
    for x in xs[1:]:
        total = total + x.astype(F32)
    return total.astype(BF)


def gather(own, axis):
    bits = lax.axis_size(axis).bit_length() - 1
    held = own
    for bit in reversed(range(2, bits)):
        got = swap(held, axis, bit)
        n, w = own.shape
        held = jnp.concatenate([held.reshape(-1, 1, n, w), got.reshape(-1, 1, n, w)], axis=1).reshape(-1, w)
    two = swap(held, axis, 1)
    one = swap(held, axis, 0)
    three = swap(two, axis, 0)
    return held, one, two, three


def odd(x, size):
    return x.reshape(-1, 2, size, x.shape[1])[:, 1].reshape(-1, x.shape[1])


def even(x, size):
    return x.reshape(-1, 2, size, x.shape[1])[:, 0].reshape(-1, x.shape[1])


def scatter_rest(terms, axis, size):
    bits = lax.axis_size(axis).bit_length() - 1
    for bit in range(2, bits):
        got = swap(add(*[odd(t, size) for t in terms]), axis, bit)
        terms = [even(t, size) for t in terms] + [got]
    return terms


def body(
    rhs_low,
    rhs_top,
    lower_blocks,
    upper_blocks,
    block_target,
    inv_lower_low,
    inv_upper_low,
    inv_lower_top,
    inv_upper_top,
):
    own, width, _ = inv_lower_low.shape
    rows, cols = lax.axis_size("row"), lax.axis_size("col")
    tops = inv_lower_top.shape[0]
    own_top = tops // cols
    ids = jnp.stack([lax.axis_index("row"), lax.axis_index("col")]).astype(jnp.int32)
    targets = block_target.T

    fwds = solve_fwd(inv_lower_low, rhs_low, CHUNKS)
    got = [gather(fwd, "row") for fwd in fwds]
    mat_l = sum_blocks(True, ids, targets, lower_blocks, rows, tops, own)
    mat_u = sum_blocks(False, ids, targets, upper_blocks, rows, tops, own)
    sol_top = sol_low = None
    solved = []
    for i in range(CHUNKS):
        three, one, two, zero = apply_lower(mat_l, got[i])
        xa = swap(three, "col", 0)
        xb = swap(one, "col", 0)
        z1 = swap(add(two, xa), "col", 1)
        terms = scatter_rest([zero, xb, z1], "col", own_top * width)
        sol_top, sol = solve_top(ids, rhs_top, inv_lower_top, inv_upper_top, terms, sol_top, i, CHUNKS)
        solved.append(gather(sol, "col"))
    for i in range(CHUNKS):
        first, two, zero = apply_upper(mat_u, solved[i])
        per = two.shape[0]
        core = swap(first, "row", 0)
        yy = swap(add(two, core[:per]), "row", 1)
        if rows == 4:
            terms = [(zero, 0), (core, 1), (yy, 0)]
        else:
            terms = [(t, 0) for t in scatter_rest([zero, core[per:], yy], "row", own * width)]
        sol_low = solve_low(inv_upper_low, fwds[i], terms, sol_low, i, CHUNKS)
    return sol_low, sol_top


def solution(mesh):
    placed = (
        P(("row", "col"), None),
        P("row", None),
        P("row", "col", None, None),
        P("row", "col", None, None),
        P("row", "col"),
        P(("row", "col"), None, None),
        P(("row", "col"), None, None),
        P("row", None, None),
        P("row", None, None),
    )
    return jax.shard_map(
        body,
        mesh=mesh,
        in_specs=placed,
        out_specs=(P(("row", "col"), None), P(("row", "col"), None)),
        check_vma=False,
    )
```

```python
import functools

import jax
import jax.numpy as jnp
from jax import lax
from jax.experimental import pallas as pl
from jax.experimental.pallas import tpu as pltpu
from jax.sharding import PartitionSpec as P

BF = jnp.bfloat16
F32 = jnp.float32
CHUNKS = 2
FLIP = 1
MIB = 1 << 20
TINY = pl.CostEstimate(flops=1, bytes_accessed=1, transcendentals=0)


def params(mib, **kw):
    return pltpu.CompilerParams(vmem_limit_bytes=mib * MIB, **kw)


def place_of(low, high, count):
    slot = jnp.where(low == 0, 3, jnp.where(low == 3, 0, low))
    return slot * (count // 4) + high


def fwd_kernel(inv_hbm, rhs_hbm, *refs):
    outs, (inv_ref, rhs_ref, sems) = refs[:-3], refs[-3:]
    wide = rhs_ref.shape[1] // len(outs)
    first = pltpu.make_async_copy(inv_hbm, inv_ref, sems.at[0])
    second = pltpu.make_async_copy(rhs_hbm, rhs_ref, sems.at[1])
    first.start()
    second.start()
    first.wait()
    second.wait()
    own, width, _ = inv_ref.shape
    for i, out in enumerate(outs):
        for j in range(own):
            rows = slice(j * width, (j + 1) * width)
            out[rows, :] = jnp.dot(
                inv_ref[j], rhs_ref[rows, i * wide : (i + 1) * wide], preferred_element_type=F32
            ).astype(BF)


def solve_fwd(inv, rhs):
    return pl.pallas_call(
        fwd_kernel,
        in_specs=[pl.BlockSpec(memory_space=pltpu.HBM)] * 2,
        out_shape=[jax.ShapeDtypeStruct((rhs.shape[0], rhs.shape[1] // CHUNKS), BF)] * CHUNKS,
        scratch_shapes=[pltpu.VMEM(inv.shape, BF), pltpu.VMEM(rhs.shape, BF), pltpu.SemaphoreType.DMA((2,))],
        compiler_params=params(8),
        cost_estimate=TINY,
        name="fwd_low",
    )(inv, rhs)


def sum_kernel(lower, rows, tops, own, ids_ref, tgt_ref, blk_hbm, out_ref, acc_ref, blk_ref, sems):
    steps, per, count, width, _ = blk_ref.shape
    copies = [
        pltpu.make_async_copy(blk_hbm.at[pl.ds(i * per, per)], blk_ref.at[i], sems.at[i]) for i in range(steps)
    ]
    for copy in copies:
        copy.start()
    me_row, me_col = ids_ref[0], ids_ref[1]
    other = (me_row & 1) == 1
    acc_ref[...] = jnp.zeros(acc_ref.shape, F32)
    for i in range(steps):
        copies[i].wait()
        for e in range(per):
            for m in range(count):
                rel = tgt_ref[m, i * per + e] ^ me_col
                low, high = rel & 3, rel >> 2
                low = jnp.where(other & ((low == 1) | (low == 2)), 3 - low, low)
                rel_row = (m // own) ^ me_row
                blk = blk_ref[i, e, m].astype(F32)
                if lower:
                    at = pl.multiple_of(place_of(low, high, tops) * width, width)
                    lanes = slice((m % own) * width, (m % own + 1) * width)
                    acc_ref[rel_row, pl.ds(at, width), lanes] += blk
                else:
                    at = (place_of(rel_row & 3, rel_row >> 2, rows) * own + m % own) * width
                    acc_ref[4 * high + low, pl.ds(pl.multiple_of(at, width), width), :] += blk
    for i in range(out_ref.shape[0]):
        out_ref[i] = acc_ref[i].astype(BF)


def sum_blocks(lower, ids, targets, blocks, rows, tops, own):
    slots, count, width, _ = blocks.shape
    steps = 4
    shape = (rows, tops * width, own * width) if lower else (tops, rows * own * width, width)
    return pl.pallas_call(
        functools.partial(sum_kernel, lower, rows, tops, own),
        in_specs=[
            pl.BlockSpec(memory_space=pltpu.SMEM),
            pl.BlockSpec(memory_space=pltpu.SMEM),
            pl.BlockSpec(memory_space=pltpu.HBM),
        ],
        out_shape=jax.ShapeDtypeStruct(shape, BF),
        scratch_shapes=[
            pltpu.VMEM(shape, F32),
            pltpu.VMEM((steps, slots // steps, count, width, width), BF),
            pltpu.SemaphoreType.DMA((steps,)),
        ],
        compiler_params=params(48),
        cost_estimate=TINY,
        name="sum_lower" if lower else "sum_upper",
    )(ids, targets, blocks)


def pick_kernel(apart, ids_ref, rhs_hbm, low_hbm, up_hbm, rhs_ref, low_ref, up_ref, sems):
    width = low_ref.shape[1]
    copies = []
    for k in range(2):
        at = ids_ref[1] ^ (k * apart)
        for n, (src, dst) in enumerate(
            [
                (rhs_hbm.at[pl.ds(pl.multiple_of(at * width, width), width)], rhs_ref.at[pl.ds(k * width, width)]),
                (low_hbm.at[at], low_ref.at[k]),
                (up_hbm.at[at], up_ref.at[k]),
            ]
        ):
            copies.append(pltpu.make_async_copy(src, dst, sems.at[3 * k + n]))
    for copy in copies:
        copy.start()
    for copy in copies:
        copy.wait()


def pick_top(ids, rhs_top, inv_low, inv_up, apart):
    _, width, _ = inv_low.shape
    return pl.pallas_call(
        functools.partial(pick_kernel, apart),
        in_specs=[pl.BlockSpec(memory_space=pltpu.SMEM)] + [pl.BlockSpec(memory_space=pltpu.HBM)] * 3,
        out_shape=[
            jax.ShapeDtypeStruct((2 * width, rhs_top.shape[1]), BF),
            jax.ShapeDtypeStruct((2, width, width), BF),
            jax.ShapeDtypeStruct((2, width, width), BF),
        ],
        scratch_shapes=[pltpu.SemaphoreType.DMA((6,))],
        compiler_params=params(8),
        cost_estimate=TINY,
        name="pick_top",
    )(ids, rhs_top, inv_low, inv_up)


def put(i, value, flip, first, two, zero):
    per = two.shape[0]
    if i == 0:
        first[:per, :] = value
    elif i == 3:
        zero[...] = value
    elif (i == 1) == (flip == 0):
        first[per:, :] = value
    else:
        two[...] = value


def lower_kernel(flip, mat_ref, p0, p1, p2, p3, first, two, zero):
    pieces = (p0, p1, p2, p3)
    per = two.shape[0]
    deep = mat_ref.shape[2]
    for i in range(4):
        total = None
        for s in range(mat_ref.shape[0]):
            part = jnp.dot(
                mat_ref[s, i * per : (i + 1) * per, :],
                pieces[s % 4][(s // 4) * deep : (s // 4 + 1) * deep, :],
                preferred_element_type=F32,
            )
            total = part if total is None else total + part
        put(i, total.astype(BF), flip, first, two, zero)


def upper_kernel(flip, mat_ref, near_ref, far_ref, first, two, zero):
    half = near_ref.shape[0] // 2
    pieces = [near_ref.at[:half], far_ref.at[:half], near_ref.at[half:], far_ref.at[half:]]
    if flip:
        pieces[1], pieces[2] = pieces[2], pieces[1]
    per = two.shape[0]
    groups = mat_ref.shape[0] // 4
    for i in range(4):
        total = None
        for g in range(4):
            left = jnp.concatenate(
                [mat_ref[g + 4 * h, i * per : (i + 1) * per, :] for h in range(groups)], axis=1
            )
            part = jnp.dot(left, pieces[g][...], preferred_element_type=F32)
            total = part if total is None else total + part
        put(i, total.astype(BF), 0, first, two, zero)


def apply(kernel, mat, pieces, name):
    rows, cols = mat.shape[1], pieces[0].shape[1]
    return pl.pallas_call(
        kernel,
        out_shape=[
            jax.ShapeDtypeStruct((rows // 2, cols), BF),
            jax.ShapeDtypeStruct((rows // 4, cols), BF),
            jax.ShapeDtypeStruct((rows // 4, cols), BF),
        ],
        compiler_params=params(32 if mat.size * 2 > 4 * MIB else 10),
        name=name,
    )(mat, *pieces)


def top_kernel(rhs_ref, low_ref, up_ref, mine_ref, got_ref, *refs):
    out, copy = refs[-2:]
    width = low_ref.shape[1]
    for k in range(2):
        rows, cross = slice(k * width, (k + 1) * width), slice((1 - k) * width, (2 - k) * width)
        lsum = mine_ref[rows, :].astype(F32) + got_ref[cross, :].astype(F32)
        resid = (rhs_ref[rows, :].astype(F32) - lsum).astype(BF)
        fwd = jnp.dot(low_ref[k], resid, preferred_element_type=F32).astype(BF)
        sol = jnp.dot(up_ref[k], fwd, preferred_element_type=F32).astype(BF)
        copy[rows, :] = sol
        if k == 0:
            out[...] = sol


def solve_top(picked, mine, got, into, chunk, chunks):
    rhs, inv_low, inv_up = picked
    rows, cols = mine.shape
    more = [] if into is None else [into]
    return pl.pallas_call(
        top_kernel,
        grid=(1,),
        in_specs=[
            pl.BlockSpec((rows, cols), lambda i: (0, chunk)),
            pl.BlockSpec(inv_low.shape, lambda i: (0, 0, 0)),
            pl.BlockSpec(inv_up.shape, lambda i: (0, 0, 0)),
            pl.BlockSpec((rows, cols), lambda i: (0, 0)),
            pl.BlockSpec((rows, cols), lambda i: (0, 0)),
        ]
        + [pl.BlockSpec(memory_space=pl.ANY)] * len(more),
        out_specs=[
            pl.BlockSpec((rows // 2, cols), lambda i: (0, chunk)),
            pl.BlockSpec((rows, cols), lambda i: (0, 0)),
        ],
        out_shape=[
            jax.ShapeDtypeStruct((rows // 2, cols * chunks), BF),
            jax.ShapeDtypeStruct((rows, cols), BF),
        ],
        input_output_aliases={5: 0} if more else {},
        compiler_params=params(8),
        cost_estimate=TINY,
        name="solve_top",
    )(rhs, inv_low, inv_up, mine, got, *more)


def low_kernel(parts, inv_ref, fwd_ref, *refs):
    terms, out = refs[:parts], refs[-1]
    own, width, _ = inv_ref.shape
    for j in range(own):
        rows = slice(j * width, (j + 1) * width)
        usum = terms[0][rows, :].astype(F32)
        for term in terms[1:]:
            usum = usum + term[rows, :].astype(F32)
        resid = (fwd_ref[rows, :].astype(F32) - usum).astype(BF)
        out[rows, :] = jnp.dot(inv_ref[j], resid, preferred_element_type=F32).astype(BF)


def solve_low(inv, fwd, terms, into, chunk, chunks):
    rows, cols = fwd.shape
    more = [] if into is None else [into]
    return pl.pallas_call(
        functools.partial(low_kernel, len(terms)),
        grid=(1,),
        in_specs=[
            pl.BlockSpec(inv.shape, lambda i: (0, 0, 0)),
            pl.BlockSpec((rows, cols), lambda i: (0, 0)),
        ]
        + [pl.BlockSpec((rows, cols), lambda i, at=at: (at, 0)) for _, at in terms]
        + [pl.BlockSpec(memory_space=pl.ANY)] * len(more),
        out_specs=pl.BlockSpec((rows, cols), lambda i: (0, chunk)),
        out_shape=jax.ShapeDtypeStruct((rows, cols * chunks), BF),
        input_output_aliases={2 + len(terms): 0} if more else {},
        compiler_params=params(8),
        cost_estimate=TINY,
        name="solve_low",
    )(inv, fwd, *[t for t, _ in terms], *more)


def swap(x, axis, bit):
    size = lax.axis_size(axis)
    return lax.ppermute(x, axis, [(i, i ^ (1 << bit)) for i in range(size)])


def cross(x, bit, flip):
    rows, cols = lax.axis_size("row"), lax.axis_size("col")
    pairs = [(r * cols + c, r * cols + (c ^ (1 << (bit ^ flip ^ (r & 1))))) for r in range(rows) for c in range(cols)]
    return lax.ppermute(x, ("row", "col"), pairs)


def add(*xs):
    total = xs[0].astype(F32)
    for x in xs[1:]:
        total = total + x.astype(F32)
    return total.astype(BF)


def weave(x, y, size):
    w = x.shape[1]
    return jnp.concatenate([x.reshape(-1, 1, size, w), y.reshape(-1, 1, size, w)], axis=1).reshape(-1, w)


def odd(x, size):
    return x.reshape(-1, 2, size, x.shape[1])[:, 1].reshape(-1, x.shape[1])


def even(x, size):
    return x.reshape(-1, 2, size, x.shape[1])[:, 0].reshape(-1, x.shape[1])


def after(x, *done):
    return lax.optimization_barrier((x, *done))[0]


def far_row(own):
    held = own
    for bit in reversed(range(2, lax.axis_size("row").bit_length() - 1)):
        held = weave(held, swap(held, "row", bit), own.shape[0])
    return held, swap(held, "row", 1)


def sums_col(terms, size):
    for bit in range(2, lax.axis_size("col").bit_length() - 2):
        new = swap(add(*[odd(t, size) for t in terms]), "col", bit)
        terms = [even(t, size) for t in terms] + [new]
    return add(*terms)


def widen_col(held, size):
    for bit in reversed(range(2, lax.axis_size("col").bit_length() - 2)):
        held = weave(held, swap(held, "col", bit), size)
    return held


def sums_row(zero, core, more, size):
    per = zero.shape[0]
    if per == size:
        return [(zero, 0), (core, 1), (more, 0)]
    terms = [zero, core[per:], more]
    for bit in range(2, lax.axis_size("row").bit_length() - 1):
        new = swap(add(*[odd(t, size) for t in terms]), "row", bit)
        terms = [even(t, size) for t in terms] + [new]
    return [(t, 0) for t in terms]


def body(
    rhs_low,
    rhs_top,
    lower_blocks,
    upper_blocks,
    block_target,
    inv_lower_low,
    inv_upper_low,
    inv_lower_top,
    inv_upper_top,
):
    own, width, _ = inv_lower_low.shape
    rows, cols = lax.axis_size("row"), lax.axis_size("col")
    tops = inv_lower_top.shape[0]
    assert tops == cols and rows >= 4 and cols >= 8
    last = cols.bit_length() - 2
    ids = jnp.stack([lax.axis_index("row"), lax.axis_index("col")]).astype(jnp.int32)
    targets = block_target.T

    fwds = solve_fwd(inv_lower_low, rhs_low)
    near, far = zip(*[far_row(fwd) for fwd in fwds])
    side = [swap(x, "row", 0) for x in near]
    mat_l = sum_blocks(True, ids, targets, lower_blocks, rows, tops, own)
    far_side = [swap(after(x, mat_l), "row", 0) for x in far]
    flips = [i % 2 * FLIP for i in range(CHUNKS)]
    parts = [
        apply(functools.partial(lower_kernel, flip), mat_l, pieces, "apply_lower")
        for flip, pieces in zip(flips, zip(near, side, far, far_side))
    ]
    mat_u = sum_blocks(False, after(ids, parts[-1][0]), targets, upper_blocks, rows, tops, own)
    picked = pick_top(ids, rhs_top, inv_lower_top, inv_upper_top, cols // 2)
    sol_top = sol_low = None
    solved = []
    for i, (flip, (first, two, zero)) in enumerate(zip(flips, parts)):
        got = after(cross(first, 0, flip), mat_u)
        more = cross(add(two, got[: two.shape[0]]), 1, flip)
        mine = sums_col([zero, got[two.shape[0] :], more], width)
        other = swap(mine, "col", last)
        sol_top, both = solve_top(picked, mine, other, sol_top, i, CHUNKS)
        held = widen_col(both, width)
        held = jnp.concatenate([held, cross(held, 1, flip)], axis=0)
        solved.append((held, cross(held, 0, flip)))
    for i, (flip, pieces) in enumerate(zip(flips, solved)):
        first, two, zero = apply(functools.partial(upper_kernel, flip), mat_u, pieces, "apply_upper")
        core = swap(first, "row", 0)
        more = swap(add(two, core[: two.shape[0]]), "row", 1)
        terms = sums_row(zero, core, more, own * width)
        sol_low = solve_low(inv_upper_low, fwds[i], terms, sol_low, i, CHUNKS)
    return sol_low, sol_top


def solution(mesh):
    placed = (
        P(("row", "col"), None),
        P("row", None),
        P("row", "col", None, None),
        P("row", "col", None, None),
        P("row", "col"),
        P(("row", "col"), None, None),
        P(("row", "col"), None, None),
        P("row", None, None),
        P("row", None, None),
    )
    return jax.shard_map(
        body,
        mesh=mesh,
        in_specs=placed,
        out_specs=(P(("row", "col"), None), P(("row", "col"), None)),
        check_vma=False,
    )
```

```python
import functools

import jax
import jax.numpy as jnp
from jax import lax
from jax.experimental import pallas as pl
from jax.experimental.pallas import tpu as pltpu
from jax.sharding import PartitionSpec as P

BF = jnp.bfloat16
F32 = jnp.float32
FLIPS = (0, 1)
MIB = 1 << 20


def params(mib, **kw):
    return pltpu.CompilerParams(vmem_limit_bytes=mib * MIB, **kw)


def place_of(low, high, count):
    slot = jnp.where(low == 0, 3, jnp.where(low == 3, 0, low))
    return slot * (count // 4) + high


def fwd_kernel(inv_hbm, rhs_hbm, *refs):
    outs, (inv_ref, rhs_ref, sems) = refs[:-3], refs[-3:]
    wide = rhs_ref.shape[1] // len(outs)
    first = pltpu.make_async_copy(inv_hbm, inv_ref, sems.at[0])
    second = pltpu.make_async_copy(rhs_hbm, rhs_ref, sems.at[1])
    first.start()
    second.start()
    first.wait()
    second.wait()
    own, width, _ = inv_ref.shape
    for i, out in enumerate(outs):
        for j in range(own):
            rows = slice(j * width, (j + 1) * width)
            out[rows, :] = jnp.dot(
                inv_ref[j], rhs_ref[rows, i * wide : (i + 1) * wide], preferred_element_type=F32
            ).astype(BF)


def solve_fwd(inv, rhs):
    return pl.pallas_call(
        fwd_kernel,
        in_specs=[pl.BlockSpec(memory_space=pltpu.HBM)] * 2,
        out_shape=[jax.ShapeDtypeStruct((rhs.shape[0], rhs.shape[1] // len(FLIPS)), BF)] * len(FLIPS),
        scratch_shapes=[pltpu.VMEM(inv.shape, BF), pltpu.VMEM(rhs.shape, BF), pltpu.SemaphoreType.DMA((2,))],
        compiler_params=params(8),
        name="fwd_low",
    )(inv, rhs)


def sum_kernel(lower, rows, tops, own, ids_ref, tgt_ref, blk_hbm, out_ref, acc_ref, blk_ref, sems):
    steps, per, count, width, _ = blk_ref.shape
    copies = [
        pltpu.make_async_copy(blk_hbm.at[pl.ds(i * per, per)], blk_ref.at[i], sems.at[i]) for i in range(steps)
    ]
    for copy in copies:
        copy.start()
    me_row, me_col = ids_ref[0], ids_ref[1]
    other = (me_row & 1) == 1
    acc_ref[...] = jnp.zeros(acc_ref.shape, F32)
    for i in range(steps):
        copies[i].wait()
        for e in range(per):
            for m in range(count):
                rel = tgt_ref[m, i * per + e] ^ me_col
                low, high = rel & 3, rel >> 2
                low = jnp.where(other & ((low == 1) | (low == 2)), 3 - low, low)
                rel_row = (m // own) ^ me_row
                blk = blk_ref[i, e, m].astype(F32)
                if lower:
                    at = pl.multiple_of(place_of(low, high, tops) * width, width)
                    lanes = slice((m % own) * width, (m % own + 1) * width)
                    acc_ref[rel_row, pl.ds(at, width), lanes] += blk
                else:
                    at = (place_of(rel_row & 3, rel_row >> 2, rows) * own + m % own) * width
                    acc_ref[4 * high + low, pl.ds(pl.multiple_of(at, width), width), :] += blk
    for i in range(out_ref.shape[0]):
        out_ref[i] = acc_ref[i].astype(BF)


def sum_blocks(lower, ids, targets, blocks, rows, tops, own):
    slots, count, width, _ = blocks.shape
    steps = 4
    shape = (rows, tops * width, own * width) if lower else (tops, rows * own * width, width)
    return pl.pallas_call(
        functools.partial(sum_kernel, lower, rows, tops, own),
        in_specs=[
            pl.BlockSpec(memory_space=pltpu.SMEM),
            pl.BlockSpec(memory_space=pltpu.SMEM),
            pl.BlockSpec(memory_space=pltpu.HBM),
        ],
        out_shape=jax.ShapeDtypeStruct(shape, BF),
        scratch_shapes=[
            pltpu.VMEM(shape, F32),
            pltpu.VMEM((steps, slots // steps, count, width, width), BF),
            pltpu.SemaphoreType.DMA((steps,)),
        ],
        compiler_params=params(48),
        name="sum_lower" if lower else "sum_upper",
    )(ids, targets, blocks)


def pick_kernel(apart, ids_ref, rhs_hbm, low_hbm, up_hbm, rhs_ref, low_ref, up_ref, sems):
    width = low_ref.shape[1]
    copies = []
    for k in range(2):
        at = ids_ref[1] ^ (k * apart)
        for n, (src, dst) in enumerate(
            [
                (rhs_hbm.at[pl.ds(pl.multiple_of(at * width, width), width)], rhs_ref.at[pl.ds(k * width, width)]),
                (low_hbm.at[at], low_ref.at[k]),
                (up_hbm.at[at], up_ref.at[k]),
            ]
        ):
            copies.append(pltpu.make_async_copy(src, dst, sems.at[3 * k + n]))
    for copy in copies:
        copy.start()
    for copy in copies:
        copy.wait()


def pick_top(ids, rhs_top, inv_low, inv_up, apart):
    _, width, _ = inv_low.shape
    return pl.pallas_call(
        functools.partial(pick_kernel, apart),
        in_specs=[pl.BlockSpec(memory_space=pltpu.SMEM)] + [pl.BlockSpec(memory_space=pltpu.HBM)] * 3,
        out_shape=[
            jax.ShapeDtypeStruct((2 * width, rhs_top.shape[1]), BF),
            jax.ShapeDtypeStruct((2, width, width), BF),
            jax.ShapeDtypeStruct((2, width, width), BF),
        ],
        scratch_shapes=[pltpu.SemaphoreType.DMA((6,))],
        compiler_params=params(8),
        name="pick_top",
    )(ids, rhs_top, inv_low, inv_up)


def lower_kernel(begin, mat_ref, p0, p1, p2, p3, *outs):
    pieces = (p0, p1, p2, p3)
    per = outs[0].shape[0]
    deep = mat_ref.shape[2]
    for i, out in enumerate(outs, begin):
        total = None
        for s in range(mat_ref.shape[0]):
            part = jnp.dot(
                mat_ref[s, i * per : (i + 1) * per, :],
                pieces[s % 4][(s // 4) * deep : (s // 4 + 1) * deep, :],
                preferred_element_type=F32,
            )
            total = part if total is None else total + part
        out[...] = total.astype(BF)


def upper_kernel(begin, mat_ref, p0, p1, p2, p3, *outs):
    pieces = (p0, p1, p2, p3)
    per = outs[0].shape[0]
    groups = mat_ref.shape[0] // 4
    for i, out in enumerate(outs, begin):
        total = None
        for g in range(4):
            left = jnp.concatenate(
                [mat_ref[g + 4 * h, i * per : (i + 1) * per, :] for h in range(groups)], axis=1
            )
            part = jnp.dot(left, pieces[g][...], preferred_element_type=F32)
            total = part if total is None else total + part
        out[...] = total.astype(BF)


def apply(kernel, mat, pieces, begin, end, name):
    rows, cols = mat.shape[1], pieces[0].shape[1]
    return pl.pallas_call(
        functools.partial(kernel, begin),
        out_shape=[jax.ShapeDtypeStruct((rows // 4, cols), BF)] * (end - begin),
        compiler_params=params(32 if mat.size * 2 > 4 * MIB else 10),
        name=name,
    )(mat, *pieces)


def top_kernel(rhs_ref, low_ref, up_ref, mine_ref, got_ref, out_ref):
    width = low_ref.shape[1]
    for k in range(2):
        rows, cross = slice(k * width, (k + 1) * width), slice((1 - k) * width, (2 - k) * width)
        lsum = mine_ref[rows, :].astype(F32) + got_ref[cross, :].astype(F32)
        resid = (rhs_ref[rows, :].astype(F32) - lsum).astype(BF)
        fwd = jnp.dot(low_ref[k], resid, preferred_element_type=F32).astype(BF)
        out_ref[rows, :] = jnp.dot(up_ref[k], fwd, preferred_element_type=F32).astype(BF)


def solve_top(picked, mine, got, chunk):
    rhs, inv_low, inv_up = picked
    rows, cols = mine.shape
    return pl.pallas_call(
        top_kernel,
        grid=(1,),
        in_specs=[
            pl.BlockSpec((rows, cols), lambda i: (0, chunk)),
            pl.BlockSpec(inv_low.shape, lambda i: (0, 0, 0)),
            pl.BlockSpec(inv_up.shape, lambda i: (0, 0, 0)),
            pl.BlockSpec((rows, cols), lambda i: (0, 0)),
            pl.BlockSpec((rows, cols), lambda i: (0, 0)),
        ],
        out_specs=pl.BlockSpec((rows, cols), lambda i: (0, 0)),
        out_shape=jax.ShapeDtypeStruct((rows, cols), BF),
        compiler_params=params(8),
        name="solve_top",
    )(rhs, inv_low, inv_up, mine, got)


def low_kernel(parts, inv_ref, fwd_ref, *refs):
    terms, out = refs[:parts], refs[-1]
    own, width, _ = inv_ref.shape
    for j in range(own):
        rows = slice(j * width, (j + 1) * width)
        usum = terms[0][rows, :].astype(F32)
        for term in terms[1:]:
            usum = usum + term[rows, :].astype(F32)
        resid = (fwd_ref[rows, :].astype(F32) - usum).astype(BF)
        out[rows, :] = jnp.dot(inv_ref[j], resid, preferred_element_type=F32).astype(BF)


def solve_low(inv, fwd, terms, into, chunk, chunks):
    rows, cols = fwd.shape
    more = [] if into is None else [into]
    return pl.pallas_call(
        functools.partial(low_kernel, len(terms)),
        grid=(1,),
        in_specs=[
            pl.BlockSpec(inv.shape, lambda i: (0, 0, 0)),
            pl.BlockSpec((rows, cols), lambda i: (0, 0)),
        ]
        + [pl.BlockSpec((rows, cols), lambda i: (0, 0))] * len(terms)
        + [pl.BlockSpec(memory_space=pl.ANY)] * len(more),
        out_specs=pl.BlockSpec((rows, cols), lambda i: (0, chunk)),
        out_shape=jax.ShapeDtypeStruct((rows, cols * chunks), BF),
        input_output_aliases={2 + len(terms): 0} if more else {},
        compiler_params=params(8),
        name="solve_low",
    )(inv, fwd, *terms, *more)


def swap(x, axis, bit):
    size = lax.axis_size(axis)
    return lax.ppermute(x, axis, [(i, i ^ (1 << bit)) for i in range(size)])


def cross(x, bit, flip):
    rows, cols = lax.axis_size("row"), lax.axis_size("col")
    pairs = [(r * cols + c, r * cols + (c ^ (1 << (bit ^ flip ^ (r & 1))))) for r in range(rows) for c in range(cols)]
    return lax.ppermute(x, ("row", "col"), pairs)


def add(*xs):
    total = xs[0].astype(F32)
    for x in xs[1:]:
        total = total + x.astype(F32)
    return total.astype(BF)


def weave(x, y, size):
    w = x.shape[1]
    return jnp.concatenate([x.reshape(-1, 1, size, w), y.reshape(-1, 1, size, w)], axis=1).reshape(-1, w)


def odd(x, size):
    return x.reshape(-1, 2, size, x.shape[1])[:, 1].reshape(-1, x.shape[1])


def even(x, size):
    return x.reshape(-1, 2, size, x.shape[1])[:, 0].reshape(-1, x.shape[1])


def after(x, *done):
    return lax.optimization_barrier((x, *done))[0]


def far_row(own):
    held = own
    for bit in reversed(range(2, lax.axis_size("row").bit_length() - 1)):
        held = weave(held, swap(held, "row", bit), own.shape[0])
    return held, swap(held, "row", 1)


def sums_col(terms, size):
    for bit in range(2, lax.axis_size("col").bit_length() - 2):
        new = swap(add(*[odd(t, size) for t in terms]), "col", bit)
        terms = [even(t, size) for t in terms] + [new]
    return add(*terms)


def widen_col(held, size):
    for bit in reversed(range(2, lax.axis_size("col").bit_length() - 2)):
        held = weave(held, swap(held, "col", bit), size)
    return held


def sums_row(terms, size):
    for bit in range(2, lax.axis_size("row").bit_length() - 1):
        new = swap(add(*[odd(t, size) for t in terms]), "row", bit)
        terms = [even(t, size) for t in terms] + [new]
    return terms


def body(
    rhs_low,
    rhs_top,
    lower_blocks,
    upper_blocks,
    block_target,
    inv_lower_low,
    inv_upper_low,
    inv_lower_top,
    inv_upper_top,
):
    own, width, _ = inv_lower_low.shape
    rows, cols = lax.axis_size("row"), lax.axis_size("col")
    tops = inv_lower_top.shape[0]
    assert tops == cols and rows >= 4 and cols >= 8
    last = cols.bit_length() - 2
    ids = jnp.stack([lax.axis_index("row"), lax.axis_index("col")]).astype(jnp.int32)
    targets = block_target.T

    fwds = solve_fwd(inv_lower_low, rhs_low)
    near, far = zip(*[far_row(fwd) for fwd in fwds])
    side = [swap(x, "row", 0) for x in near]
    mat_l = sum_blocks(True, ids, targets, lower_blocks, rows, tops, own)
    far_side = [swap(after(x, mat_l), "row", 0) for x in far]
    pieces = list(zip(near, side, far, far_side))
    parts = [apply(lower_kernel, mat_l, p, 0, 1, "first_lower") for p in pieces]
    parts = [x + apply(lower_kernel, mat_l, p, 1, 4, "apply_lower") for x, p in zip(parts, pieces)]
    mine = []
    for i, (three, one, two, zero) in enumerate(parts):
        flip = FLIPS[i]
        if flip:
            one, two = two, one
        got = cross(three, 0, flip)
        rest = cross(one, 0, flip)
        more = cross(add(two, got), 1, flip)
        mine.append(sums_col([zero, rest, more], width))
    other = [swap(x, "col", last) for x in mine]
    mat_u = sum_blocks(False, after(ids, mine[-1]), targets, upper_blocks, rows, tops, own)
    picked = pick_top(after(ids, mat_u), rhs_top, inv_lower_top, inv_upper_top, cols // 2)
    sol_low = None
    top_parts, solved = [], []
    for i, flip in enumerate(FLIPS):
        both = solve_top(picked, mine[i], other[i], i)
        top_parts.append(both[:width])
        zero = widen_col(both, width)
        two = cross(zero, 1, flip)
        one = cross(zero, 0, flip)
        three = cross(two, 0, flip)
        if flip:
            one, two = two, one
        solved.append((zero, one, two, three))
    for i, pieces in enumerate(solved):
        (three,) = apply(upper_kernel, mat_u, pieces, 0, 1, "first_upper")
        one, two, zero = apply(upper_kernel, mat_u, pieces, 1, 4, "apply_upper")
        got, rest = swap(three, "row", 0), swap(one, "row", 0)
        more = swap(add(two, got), "row", 1)
        terms = sums_row([zero, rest, more], own * width)
        sol_low = solve_low(inv_upper_low, fwds[i], terms, sol_low, i, len(FLIPS))
    return sol_low, jnp.concatenate(top_parts, axis=1)


def solution(mesh):
    placed = (
        P(("row", "col"), None),
        P("row", None),
        P("row", "col", None, None),
        P("row", "col", None, None),
        P("row", "col"),
        P(("row", "col"), None, None),
        P(("row", "col"), None, None),
        P("row", None, None),
        P("row", None, None),
    )
    return jax.shard_map(
        body,
        mesh=mesh,
        in_specs=placed,
        out_specs=(P(("row", "col"), None), P(("row", "col"), None)),
        check_vma=False,
    )
```

```python
import functools

import jax
import jax.numpy as jnp
from jax import lax
from jax.experimental import pallas as pl
from jax.experimental.pallas import tpu as pltpu
from jax.sharding import PartitionSpec as P

BF = jnp.bfloat16
F32 = jnp.float32
FLIPS = (0, 0)
MIB = 1 << 20


def params(mib, **kw):
    return pltpu.CompilerParams(vmem_limit_bytes=mib * MIB, **kw)


def place_of(low, high, count):
    slot = jnp.where(low == 0, 3, jnp.where(low == 3, 0, low))
    return slot * (count // 4) + high


def fwd_kernel(inv_hbm, rhs_hbm, *refs):
    outs, (inv_ref, rhs_ref, sems) = refs[:-3], refs[-3:]
    wide = rhs_ref.shape[1] // len(outs)
    first = pltpu.make_async_copy(inv_hbm, inv_ref, sems.at[0])
    second = pltpu.make_async_copy(rhs_hbm, rhs_ref, sems.at[1])
    first.start()
    second.start()
    first.wait()
    second.wait()
    own, width, _ = inv_ref.shape
    for i, out in enumerate(outs):
        for j in range(own):
            rows = slice(j * width, (j + 1) * width)
            out[rows, :] = jnp.dot(
                inv_ref[j], rhs_ref[rows, i * wide : (i + 1) * wide], preferred_element_type=F32
            ).astype(BF)


def solve_fwd(inv, rhs):
    return pl.pallas_call(
        fwd_kernel,
        in_specs=[pl.BlockSpec(memory_space=pltpu.HBM)] * 2,
        out_shape=[jax.ShapeDtypeStruct((rhs.shape[0], rhs.shape[1] // len(FLIPS)), BF)] * len(FLIPS),
        scratch_shapes=[pltpu.VMEM(inv.shape, BF), pltpu.VMEM(rhs.shape, BF), pltpu.SemaphoreType.DMA((2,))],
        compiler_params=params(8),
        name="fwd_low",
    )(inv, rhs)


def sum_kernel(lower, rows, tops, own, ids_ref, tgt_ref, blk_hbm, out_ref, acc_ref, blk_ref, sems):
    steps, per, count, width, _ = blk_ref.shape
    copies = [
        pltpu.make_async_copy(blk_hbm.at[pl.ds(i * per, per)], blk_ref.at[i], sems.at[i]) for i in range(steps)
    ]
    for copy in copies:
        copy.start()
    me_row, me_col = ids_ref[0], ids_ref[1]
    other = (me_row & 1) == 1
    acc_ref[...] = jnp.zeros(acc_ref.shape, F32)
    for i in range(steps):
        copies[i].wait()
        for e in range(per):
            for m in range(count):
                rel = tgt_ref[m, i * per + e] ^ me_col
                low, high = rel & 3, rel >> 2
                low = jnp.where(other & ((low == 1) | (low == 2)), 3 - low, low)
                rel_row = (m // own) ^ me_row
                blk = blk_ref[i, e, m].astype(F32)
                if lower:
                    at = pl.multiple_of(place_of(low, high, tops) * width, width)
                    lanes = slice((m % own) * width, (m % own + 1) * width)
                    acc_ref[rel_row, pl.ds(at, width), lanes] += blk
                else:
                    at = ((((3 - rel_row) & 3) * (rows // 4) + (rel_row >> 2)) * own + m % own) * width
                    acc_ref[4 * high + low, pl.ds(pl.multiple_of(at, width), width), :] += blk
    for i in range(out_ref.shape[0]):
        out_ref[i] = acc_ref[i].astype(BF)


def sum_blocks(lower, ids, targets, blocks, rows, tops, own):
    slots, count, width, _ = blocks.shape
    steps = 4
    shape = (rows, tops * width, own * width) if lower else (tops, rows * own * width, width)
    return pl.pallas_call(
        functools.partial(sum_kernel, lower, rows, tops, own),
        in_specs=[
            pl.BlockSpec(memory_space=pltpu.SMEM),
            pl.BlockSpec(memory_space=pltpu.SMEM),
            pl.BlockSpec(memory_space=pltpu.HBM),
        ],
        out_shape=jax.ShapeDtypeStruct(shape, BF),
        scratch_shapes=[
            pltpu.VMEM(shape, F32),
            pltpu.VMEM((steps, slots // steps, count, width, width), BF),
            pltpu.SemaphoreType.DMA((steps,)),
        ],
        compiler_params=params(48),
        name="sum_lower" if lower else "sum_upper",
    )(ids, targets, blocks)


def pick_kernel(apart, ids_ref, rhs_hbm, low_hbm, up_hbm, rhs_ref, low_ref, up_ref, sems):
    width = low_ref.shape[1]
    copies = []
    for k in range(2):
        at = ids_ref[1] ^ (k * apart)
        for n, (src, dst) in enumerate(
            [
                (rhs_hbm.at[pl.ds(pl.multiple_of(at * width, width), width)], rhs_ref.at[pl.ds(k * width, width)]),
                (low_hbm.at[at], low_ref.at[k]),
                (up_hbm.at[at], up_ref.at[k]),
            ]
        ):
            copies.append(pltpu.make_async_copy(src, dst, sems.at[3 * k + n]))
    for copy in copies:
        copy.start()
    for copy in copies:
        copy.wait()


def pick_top(ids, rhs_top, inv_low, inv_up, apart):
    _, width, _ = inv_low.shape
    return pl.pallas_call(
        functools.partial(pick_kernel, apart),
        in_specs=[pl.BlockSpec(memory_space=pltpu.SMEM)] + [pl.BlockSpec(memory_space=pltpu.HBM)] * 3,
        out_shape=[
            jax.ShapeDtypeStruct((2 * width, rhs_top.shape[1]), BF),
            jax.ShapeDtypeStruct((2, width, width), BF),
            jax.ShapeDtypeStruct((2, width, width), BF),
        ],
        scratch_shapes=[pltpu.SemaphoreType.DMA((6,))],
        compiler_params=params(8),
        name="pick_top",
    )(ids, rhs_top, inv_low, inv_up)


def lower_kernel(begin, mat_ref, p0, p1, p2, p3, *outs):
    pieces = (p0, p1, p2, p3)
    per = outs[0].shape[0]
    deep = mat_ref.shape[2]
    for i, out in enumerate(outs, begin):
        total = None
        for s in range(mat_ref.shape[0]):
            part = jnp.dot(
                mat_ref[s, i * per : (i + 1) * per, :],
                pieces[s % 4][(s // 4) * deep : (s // 4 + 1) * deep, :],
                preferred_element_type=F32,
            )
            total = part if total is None else total + part
        out[...] = total.astype(BF)


def upper_kernel(begin, mat_ref, p0, p1, p2, p3, *outs):
    pieces = (p0, p1, p2, p3)
    per = outs[0].shape[0]
    groups = mat_ref.shape[0] // 4
    for i, out in enumerate(outs, begin):
        total = None
        for g in range(4):
            left = jnp.concatenate(
                [mat_ref[g + 4 * h, i * per : (i + 1) * per, :] for h in range(groups)], axis=1
            )
            part = jnp.dot(left, pieces[g][...], preferred_element_type=F32)
            total = part if total is None else total + part
        out[...] = total.astype(BF)


def apply(kernel, mat, pieces, begin, end, name):
    rows, cols = mat.shape[1], pieces[0].shape[1]
    return pl.pallas_call(
        functools.partial(kernel, begin),
        out_shape=[jax.ShapeDtypeStruct((rows // 4, cols), BF)] * (end - begin),
        compiler_params=params(32 if mat.size * 2 > 4 * MIB else 10),
        name=name,
    )(mat, *pieces)


def top_kernel(rhs_ref, low_ref, up_ref, mine_ref, got_ref, out_ref):
    width = low_ref.shape[1]
    for k in range(2):
        rows, cross = slice(k * width, (k + 1) * width), slice((1 - k) * width, (2 - k) * width)
        lsum = mine_ref[rows, :].astype(F32) + got_ref[cross, :].astype(F32)
        resid = (rhs_ref[rows, :].astype(F32) - lsum).astype(BF)
        fwd = jnp.dot(low_ref[k], resid, preferred_element_type=F32).astype(BF)
        out_ref[rows, :] = jnp.dot(up_ref[k], fwd, preferred_element_type=F32).astype(BF)


def solve_top(picked, mine, got, chunk):
    rhs, inv_low, inv_up = picked
    rows, cols = mine.shape
    return pl.pallas_call(
        top_kernel,
        grid=(1,),
        in_specs=[
            pl.BlockSpec((rows, cols), lambda i: (0, chunk)),
            pl.BlockSpec(inv_low.shape, lambda i: (0, 0, 0)),
            pl.BlockSpec(inv_up.shape, lambda i: (0, 0, 0)),
            pl.BlockSpec((rows, cols), lambda i: (0, 0)),
            pl.BlockSpec((rows, cols), lambda i: (0, 0)),
        ],
        out_specs=pl.BlockSpec((rows, cols), lambda i: (0, 0)),
        out_shape=jax.ShapeDtypeStruct((rows, cols), BF),
        compiler_params=params(8),
        name="solve_top",
    )(rhs, inv_low, inv_up, mine, got)


def low_kernel(parts, inv_ref, fwd_ref, *refs):
    terms, out = refs[:parts], refs[-1]
    own, width, _ = inv_ref.shape
    for j in range(own):
        rows = slice(j * width, (j + 1) * width)
        usum = terms[0][rows, :].astype(F32)
        for term in terms[1:]:
            usum = usum + term[rows, :].astype(F32)
        resid = (fwd_ref[rows, :].astype(F32) - usum).astype(BF)
        out[rows, :] = jnp.dot(inv_ref[j], resid, preferred_element_type=F32).astype(BF)


def solve_low(inv, fwd, terms, into, chunk, chunks):
    rows, cols = fwd.shape
    more = [] if into is None else [into]
    return pl.pallas_call(
        functools.partial(low_kernel, len(terms)),
        grid=(1,),
        in_specs=[
            pl.BlockSpec(inv.shape, lambda i: (0, 0, 0)),
            pl.BlockSpec((rows, cols), lambda i: (0, 0)),
        ]
        + [pl.BlockSpec((rows, cols), lambda i: (0, 0))] * len(terms)
        + [pl.BlockSpec(memory_space=pl.ANY)] * len(more),
        out_specs=pl.BlockSpec((rows, cols), lambda i: (0, chunk)),
        out_shape=jax.ShapeDtypeStruct((rows, cols * chunks), BF),
        input_output_aliases={2 + len(terms): 0} if more else {},
        compiler_params=params(8),
        name="solve_low",
    )(inv, fwd, *terms, *more)


def swap(x, axis, bit):
    size = lax.axis_size(axis)
    return lax.ppermute(x, axis, [(i, i ^ (1 << bit)) for i in range(size)])


def cross(x, bit, flip):
    rows, cols = lax.axis_size("row"), lax.axis_size("col")
    pairs = [(r * cols + c, r * cols + (c ^ (1 << (bit ^ flip ^ (r & 1))))) for r in range(rows) for c in range(cols)]
    return lax.ppermute(x, ("row", "col"), pairs)


def add(*xs):
    total = xs[0].astype(F32)
    for x in xs[1:]:
        total = total + x.astype(F32)
    return total.astype(BF)


def weave(x, y, size):
    w = x.shape[1]
    return jnp.concatenate([x.reshape(-1, 1, size, w), y.reshape(-1, 1, size, w)], axis=1).reshape(-1, w)


def odd(x, size):
    return x.reshape(-1, 2, size, x.shape[1])[:, 1].reshape(-1, x.shape[1])


def even(x, size):
    return x.reshape(-1, 2, size, x.shape[1])[:, 0].reshape(-1, x.shape[1])


def after(x, *done):
    return lax.optimization_barrier((x, *done))[0]


def far_row(own):
    held = own
    for bit in reversed(range(2, lax.axis_size("row").bit_length() - 1)):
        held = weave(held, swap(held, "row", bit), own.shape[0])
    return held, swap(held, "row", 1)


def sums_col(terms, size):
    for bit in range(2, lax.axis_size("col").bit_length() - 2):
        new = swap(add(*[odd(t, size) for t in terms]), "col", bit)
        terms = [even(t, size) for t in terms] + [new]
    return add(*terms)


def widen_col(held, size):
    for bit in reversed(range(2, lax.axis_size("col").bit_length() - 2)):
        held = weave(held, swap(held, "col", bit), size)
    return held


def sums_row(terms, size):
    for bit in range(2, lax.axis_size("row").bit_length() - 1):
        new = swap(add(*[odd(t, size) for t in terms]), "row", bit)
        terms = [even(t, size) for t in terms] + [new]
    return terms


def body(
    rhs_low,
    rhs_top,
    lower_blocks,
    upper_blocks,
    block_target,
    inv_lower_low,
    inv_upper_low,
    inv_lower_top,
    inv_upper_top,
):
    own, width, _ = inv_lower_low.shape
    rows, cols = lax.axis_size("row"), lax.axis_size("col")
    tops = inv_lower_top.shape[0]
    assert tops == cols and rows >= 4 and cols >= 8
    last = cols.bit_length() - 2
    ids = jnp.stack([lax.axis_index("row"), lax.axis_index("col")]).astype(jnp.int32)
    targets = block_target.T

    fwds = solve_fwd(inv_lower_low, rhs_low)
    near, far = zip(*[far_row(fwd) for fwd in fwds])
    side = [swap(x, "row", 0) for x in near]
    mat_l = sum_blocks(True, ids, targets, lower_blocks, rows, tops, own)
    far_side = [swap(after(x, mat_l), "row", 0) for x in far]
    pieces = list(zip(near, side, far, far_side))
    parts = [apply(lower_kernel, mat_l, p, 0, 1, "first_lower") for p in pieces]
    parts = [x + apply(lower_kernel, mat_l, p, 1, 4, "apply_lower") for x, p in zip(parts, pieces)]
    mine = []
    for i, (three, one, two, zero) in enumerate(parts):
        flip = FLIPS[i]
        if flip:
            one, two = two, one
        got = cross(three, 0, flip)
        rest = cross(one, 0, flip)
        more = cross(add(two, got), 1, flip)
        mine.append(sums_col([zero, rest, more], width))
    other = [swap(x, "col", last) for x in mine]
    mat_u = sum_blocks(False, after(ids, mine[-1]), targets, upper_blocks, rows, tops, own)
    picked = pick_top(after(ids, mat_u), rhs_top, inv_lower_top, inv_upper_top, cols // 2)
    sol_low = None
    top_parts, solved = [], []
    for i, flip in enumerate(FLIPS):
        both = solve_top(picked, mine[i], other[i], i)
        top_parts.append(both[:width])
        zero = widen_col(both, width)
        two = cross(zero, 1, flip)
        one = cross(zero, 0, flip)
        three = cross(two, 0, flip)
        if flip:
            one, two = two, one
        solved.append((zero, one, two, three))
    begun, sent = [], []
    for pieces in solved:
        three, two = apply(upper_kernel, mat_u, pieces, 0, 2, "first_upper")
        send = add(two, swap(three, "row", 0))
        sent.append(send)
        begun.append(swap(send, "row", 1))
    for i, pieces in enumerate(solved):
        pieces = (after(pieces[0], *sent[:]), *pieces[1:])
        one, zero = apply(upper_kernel, mat_u, pieces, 2, 4, "apply_upper")
        part = zero.astype(F32) + begun[i].astype(F32)
        terms = sums_row([part, swap(one, "row", 0)], own * width)
        sol_low = solve_low(inv_upper_low, fwds[i], terms, sol_low, i, len(FLIPS))
    top_parts[0] = after(top_parts[0], *sent)
    return sol_low, jnp.concatenate(top_parts, axis=1)


def solution(mesh):
    placed = (
        P(("row", "col"), None),
        P("row", None),
        P("row", "col", None, None),
        P("row", "col", None, None),
        P("row", "col"),
        P(("row", "col"), None, None),
        P(("row", "col"), None, None),
        P("row", None, None),
        P("row", None, None),
    )
    return jax.shard_map(
        body,
        mesh=mesh,
        in_specs=placed,
        out_specs=(P(("row", "col"), None), P(("row", "col"), None)),
        check_vma=False,
    )
```

```python
import functools

import jax
import jax.numpy as jnp
from jax import lax
from jax.experimental import pallas as pl
from jax.experimental.pallas import tpu as pltpu
from jax.sharding import PartitionSpec as P

BF = jnp.bfloat16
F32 = jnp.float32
FLIPS = (0, 0)
MIB = 1 << 20


def params(mib, **kw):
    return pltpu.CompilerParams(vmem_limit_bytes=mib * MIB, **kw)


def place_of(low, high, count):
    slot = jnp.where(low == 0, 3, jnp.where(low == 3, 0, low))
    return slot * (count // 4) + high


def fwd_kernel(inv_hbm, rhs_hbm, *refs):
    outs, (inv_ref, rhs_ref, sems) = refs[:-3], refs[-3:]
    wide = rhs_ref.shape[1] // len(outs)
    first = pltpu.make_async_copy(inv_hbm, inv_ref, sems.at[0])
    second = pltpu.make_async_copy(rhs_hbm, rhs_ref, sems.at[1])
    first.start()
    second.start()
    first.wait()
    second.wait()
    own, width, _ = inv_ref.shape
    for i, out in enumerate(outs):
        for j in range(own):
            rows = slice(j * width, (j + 1) * width)
            out[rows, :] = jnp.dot(
                inv_ref[j], rhs_ref[rows, i * wide : (i + 1) * wide], preferred_element_type=F32
            ).astype(BF)


def solve_fwd(inv, rhs):
    return pl.pallas_call(
        fwd_kernel,
        in_specs=[pl.BlockSpec(memory_space=pltpu.HBM)] * 2,
        out_shape=[jax.ShapeDtypeStruct((rhs.shape[0], rhs.shape[1] // len(FLIPS)), BF)] * len(FLIPS),
        scratch_shapes=[pltpu.VMEM(inv.shape, BF), pltpu.VMEM(rhs.shape, BF), pltpu.SemaphoreType.DMA((2,))],
        compiler_params=params(8),
        name="fwd_low",
    )(inv, rhs)


def sum_kernel(lower, rows, tops, own, ids_ref, tgt_ref, blk_hbm, out_ref, acc_ref, blk_ref, sems):
    steps, per, count, width, _ = blk_ref.shape
    copies = [
        pltpu.make_async_copy(blk_hbm.at[pl.ds(i * per, per)], blk_ref.at[i], sems.at[i]) for i in range(steps)
    ]
    for copy in copies:
        copy.start()
    me_row, me_col = ids_ref[0], ids_ref[1]
    other = (me_row & 1) == 1
    acc_ref[...] = jnp.zeros(acc_ref.shape, F32)
    for i in range(steps):
        copies[i].wait()
        for e in range(per):
            for m in range(count):
                rel = tgt_ref[m, i * per + e] ^ me_col
                low, high = rel & 3, rel >> 2
                low = jnp.where(other & ((low == 1) | (low == 2)), 3 - low, low)
                rel_row = (m // own) ^ me_row
                blk = blk_ref[i, e, m].astype(F32)
                if lower:
                    at = pl.multiple_of(place_of(low, high, tops) * width, width)
                    lanes = slice((m % own) * width, (m % own + 1) * width)
                    acc_ref[rel_row, pl.ds(at, width), lanes] += blk
                else:
                    at = ((((3 - rel_row) & 3) * (rows // 4) + (rel_row >> 2)) * own + m % own) * width
                    acc_ref[4 * high + low, pl.ds(pl.multiple_of(at, width), width), :] += blk
    for i in range(out_ref.shape[0]):
        out_ref[i] = acc_ref[i].astype(BF)


def sum_blocks(lower, ids, targets, blocks, rows, tops, own):
    slots, count, width, _ = blocks.shape
    steps = 4
    shape = (rows, tops * width, own * width) if lower else (tops, rows * own * width, width)
    return pl.pallas_call(
        functools.partial(sum_kernel, lower, rows, tops, own),
        in_specs=[
            pl.BlockSpec(memory_space=pltpu.SMEM),
            pl.BlockSpec(memory_space=pltpu.SMEM),
            pl.BlockSpec(memory_space=pltpu.HBM),
        ],
        out_shape=jax.ShapeDtypeStruct(shape, BF),
        scratch_shapes=[
            pltpu.VMEM(shape, F32),
            pltpu.VMEM((steps, slots // steps, count, width, width), BF),
            pltpu.SemaphoreType.DMA((steps,)),
        ],
        compiler_params=params(48),
        name="sum_lower" if lower else "sum_upper",
    )(ids, targets, blocks)


def pick_kernel(apart, ids_ref, rhs_hbm, low_hbm, up_hbm, rhs_ref, low_ref, up_ref, sems):
    width = low_ref.shape[1]
    copies = []
    for k in range(2):
        at = ids_ref[1] ^ (k * apart)
        for n, (src, dst) in enumerate(
            [
                (rhs_hbm.at[pl.ds(pl.multiple_of(at * width, width), width)], rhs_ref.at[pl.ds(k * width, width)]),
                (low_hbm.at[at], low_ref.at[k]),
                (up_hbm.at[at], up_ref.at[k]),
            ]
        ):
            copies.append(pltpu.make_async_copy(src, dst, sems.at[3 * k + n]))
    for copy in copies:
        copy.start()
    for copy in copies:
        copy.wait()


def pick_top(ids, rhs_top, inv_low, inv_up, apart):
    _, width, _ = inv_low.shape
    return pl.pallas_call(
        functools.partial(pick_kernel, apart),
        in_specs=[pl.BlockSpec(memory_space=pltpu.SMEM)] + [pl.BlockSpec(memory_space=pltpu.HBM)] * 3,
        out_shape=[
            jax.ShapeDtypeStruct((2 * width, rhs_top.shape[1]), BF),
            jax.ShapeDtypeStruct((2, width, width), BF),
            jax.ShapeDtypeStruct((2, width, width), BF),
        ],
        scratch_shapes=[pltpu.SemaphoreType.DMA((6,))],
        compiler_params=params(8),
        name="pick_top",
    )(ids, rhs_top, inv_low, inv_up)


def lower_kernel(begin, mat_ref, p0, p1, p2, p3, *outs):
    pieces = (p0, p1, p2, p3)
    per = outs[0].shape[0]
    deep = mat_ref.shape[2]
    for i, out in enumerate(outs, begin):
        total = None
        for s in range(mat_ref.shape[0]):
            part = jnp.dot(
                mat_ref[s, i * per : (i + 1) * per, :],
                pieces[s % 4][(s // 4) * deep : (s // 4 + 1) * deep, :],
                preferred_element_type=F32,
            )
            total = part if total is None else total + part
        out[...] = total.astype(BF)


def upper_kernel(begin, mat_ref, p0, p1, p2, p3, *outs):
    pieces = (p0, p1, p2, p3)
    per = outs[0].shape[0]
    groups = mat_ref.shape[0] // 4
    for i, out in enumerate(outs, begin):
        total = None
        for g in range(4):
            left = jnp.concatenate(
                [mat_ref[g + 4 * h, i * per : (i + 1) * per, :] for h in range(groups)], axis=1
            )
            part = jnp.dot(left, pieces[g][...], preferred_element_type=F32)
            total = part if total is None else total + part
        out[...] = total.astype(BF)


def apply(kernel, mat, pieces, begin, end, name):
    rows, cols = mat.shape[1], pieces[0].shape[1]
    return pl.pallas_call(
        functools.partial(kernel, begin),
        out_shape=[jax.ShapeDtypeStruct((rows // 4, cols), BF)] * (end - begin),
        compiler_params=params(32 if mat.size * 2 > 4 * MIB else 10),
        name=name,
    )(mat, *pieces)


def top_kernel(rhs_ref, low_ref, up_ref, mine_ref, got_ref, out_ref):
    width = low_ref.shape[1]
    for k in range(2):
        rows, cross = slice(k * width, (k + 1) * width), slice((1 - k) * width, (2 - k) * width)
        lsum = mine_ref[rows, :].astype(F32) + got_ref[cross, :].astype(F32)
        resid = (rhs_ref[rows, :].astype(F32) - lsum).astype(BF)
        fwd = jnp.dot(low_ref[k], resid, preferred_element_type=F32).astype(BF)
        out_ref[rows, :] = jnp.dot(up_ref[k], fwd, preferred_element_type=F32).astype(BF)


def solve_top(picked, mine, got, chunk):
    rhs, inv_low, inv_up = picked
    rows, cols = mine.shape
    return pl.pallas_call(
        top_kernel,
        grid=(1,),
        in_specs=[
            pl.BlockSpec((rows, cols), lambda i: (0, chunk)),
            pl.BlockSpec(inv_low.shape, lambda i: (0, 0, 0)),
            pl.BlockSpec(inv_up.shape, lambda i: (0, 0, 0)),
            pl.BlockSpec((rows, cols), lambda i: (0, 0)),
            pl.BlockSpec((rows, cols), lambda i: (0, 0)),
        ],
        out_specs=pl.BlockSpec((rows, cols), lambda i: (0, 0)),
        out_shape=jax.ShapeDtypeStruct((rows, cols), BF),
        compiler_params=params(8),
        name="solve_top",
    )(rhs, inv_low, inv_up, mine, got)


def low_kernel(parts, inv_ref, fwd_ref, *refs):
    terms, out = refs[:parts], refs[-1]
    own, width, _ = inv_ref.shape
    for j in range(own):
        rows = slice(j * width, (j + 1) * width)
        usum = terms[0][rows, :].astype(F32)
        for term in terms[1:]:
            usum = usum + term[rows, :].astype(F32)
        resid = (fwd_ref[rows, :].astype(F32) - usum).astype(BF)
        out[rows, :] = jnp.dot(inv_ref[j], resid, preferred_element_type=F32).astype(BF)


def solve_low(inv, fwd, terms, into, chunk, chunks):
    rows, cols = fwd.shape
    more = [] if into is None else [into]
    return pl.pallas_call(
        functools.partial(low_kernel, len(terms)),
        grid=(1,),
        in_specs=[
            pl.BlockSpec(inv.shape, lambda i: (0, 0, 0)),
            pl.BlockSpec((rows, cols), lambda i: (0, 0)),
        ]
        + [pl.BlockSpec((rows, cols), lambda i: (0, 0))] * len(terms)
        + [pl.BlockSpec(memory_space=pl.ANY)] * len(more),
        out_specs=pl.BlockSpec((rows, cols), lambda i: (0, chunk)),
        out_shape=jax.ShapeDtypeStruct((rows, cols * chunks), BF),
        input_output_aliases={2 + len(terms): 0} if more else {},
        compiler_params=params(8),
        name="solve_low",
    )(inv, fwd, *terms, *more)


def swap(x, axis, bit):
    size = lax.axis_size(axis)
    return lax.ppermute(x, axis, [(i, i ^ (1 << bit)) for i in range(size)])


def cross(x, bit, flip):
    rows, cols = lax.axis_size("row"), lax.axis_size("col")
    pairs = [(r * cols + c, r * cols + (c ^ (1 << (bit ^ flip ^ (r & 1))))) for r in range(rows) for c in range(cols)]
    return lax.ppermute(x, ("row", "col"), pairs)


def add(*xs):
    total = xs[0].astype(F32)
    for x in xs[1:]:
        total = total + x.astype(F32)
    return total.astype(BF)


def weave(x, y, size):
    w = x.shape[1]
    return jnp.concatenate([x.reshape(-1, 1, size, w), y.reshape(-1, 1, size, w)], axis=1).reshape(-1, w)


def odd(x, size):
    return x.reshape(-1, 2, size, x.shape[1])[:, 1].reshape(-1, x.shape[1])


def even(x, size):
    return x.reshape(-1, 2, size, x.shape[1])[:, 0].reshape(-1, x.shape[1])


def after(x, *done):
    return lax.optimization_barrier((x, *done))[0]


def far_row(own):
    held = own
    for bit in reversed(range(2, lax.axis_size("row").bit_length() - 1)):
        held = weave(held, swap(held, "row", bit), own.shape[0])
    return held, swap(held, "row", 1)


def sums_col(terms, size):
    for bit in range(2, lax.axis_size("col").bit_length() - 2):
        new = swap(add(*[odd(t, size) for t in terms]), "col", bit)
        terms = [even(t, size) for t in terms] + [new]
    return add(*terms)


def widen_col(held, size):
    for bit in reversed(range(2, lax.axis_size("col").bit_length() - 2)):
        held = weave(held, swap(held, "col", bit), size)
    return held


def sums_row(terms, size):
    for bit in range(2, lax.axis_size("row").bit_length() - 1):
        new = swap(add(*[odd(t, size) for t in terms]), "row", bit)
        terms = [even(t, size) for t in terms] + [new]
    return terms


def body(
    rhs_low,
    rhs_top,
    lower_blocks,
    upper_blocks,
    block_target,
    inv_lower_low,
    inv_upper_low,
    inv_lower_top,
    inv_upper_top,
):
    own, width, _ = inv_lower_low.shape
    rows, cols = lax.axis_size("row"), lax.axis_size("col")
    tops = inv_lower_top.shape[0]
    assert tops == cols and rows >= 4 and cols >= 8
    last = cols.bit_length() - 2
    ids = jnp.stack([lax.axis_index("row"), lax.axis_index("col")]).astype(jnp.int32)
    targets = block_target.T

    fwds = solve_fwd(inv_lower_low, rhs_low)
    near, far = zip(*[far_row(fwd) for fwd in fwds])
    side = [swap(x, "row", 0) for x in near]
    mat_l = sum_blocks(True, ids, targets, lower_blocks, rows, tops, own)
    far_side = [swap(after(x, mat_l), "row", 0) for x in far]
    pieces = list(zip(near, side, far, far_side))
    parts = [apply(lower_kernel, mat_l, p, 0, 1, "first_lower") for p in pieces]
    parts = [x + apply(lower_kernel, mat_l, p, 1, 4, "apply_lower") for x, p in zip(parts, pieces)]
    mine = []
    for i, (three, one, two, zero) in enumerate(parts):
        flip = FLIPS[i]
        if flip:
            one, two = two, one
        got = cross(three, 0, flip)
        rest = cross(one, 0, flip)
        more = cross(add(two, got), 1, flip)
        mine.append(sums_col([zero, rest, more], width))
    other = [swap(x, "col", last) for x in mine]
    mat_u = sum_blocks(False, after(ids, mine[-1]), targets, upper_blocks, rows, tops, own)
    picked = pick_top(after(ids, mat_u), rhs_top, inv_lower_top, inv_upper_top, cols // 2)
    sol_low = None
    top_parts, solved = [], []
    for i, flip in enumerate(FLIPS):
        both = solve_top(picked, mine[i], other[i], i)
        top_parts.append(both[:width])
        zero = widen_col(both, width)
        two = cross(zero, 1, flip)
        one = cross(zero, 0, flip)
        three = cross(after(two, one), 0, flip)
        if flip:
            one, two = two, one
        solved.append((zero, one, two, three))
    begun, sent = [], []
    for pieces in solved:
        three, two = apply(upper_kernel, mat_u, pieces, 0, 2, "first_upper")
        send = add(two, after(swap(three, "row", 0), *begun))
        sent.append(send)
        begun.append(swap(send, "row", 1).astype(F32))
    for i, pieces in enumerate(solved):
        pieces = (after(pieces[0], *sent[: i + 1]), *pieces[1:])
        one, zero = apply(upper_kernel, mat_u, pieces, 2, 4, "apply_upper")
        part = zero.astype(F32) + begun[i]
        terms = sums_row([part, swap(one, "row", 0)], own * width)
        sol_low = solve_low(inv_upper_low, fwds[i], terms, sol_low, i, len(FLIPS))
    top_parts[0] = after(top_parts[0], *sent)
    return sol_low, jnp.concatenate(top_parts, axis=1)


def solution(mesh):
    placed = (
        P(("row", "col"), None),
        P("row", None),
        P("row", "col", None, None),
        P("row", "col", None, None),
        P("row", "col"),
        P(("row", "col"), None, None),
        P(("row", "col"), None, None),
        P("row", None, None),
        P("row", None, None),
    )
    return jax.shard_map(
        body,
        mesh=mesh,
        in_specs=placed,
        out_specs=(P(("row", "col"), None), P(("row", "col"), None)),
        check_vma=False,
    )
```

```python
import functools

import jax
import jax.numpy as jnp
from jax import lax
from jax.experimental import pallas as pl
from jax.experimental.pallas import tpu as pltpu
from jax.sharding import PartitionSpec as P

BF = jnp.bfloat16
F32 = jnp.float32
FLIPS = (0, 0)
MIB = 1 << 20


def params(mib, **kw):
    return pltpu.CompilerParams(vmem_limit_bytes=int(mib * MIB), **kw)


def place_of(low, high, count):
    slot = jnp.where(low == 0, 3, jnp.where(low == 3, 0, low))
    return slot * (count // 4) + high


def fwd_kernel(inv_hbm, rhs_hbm, *refs):
    outs, (inv_ref, rhs_ref, sems) = refs[:-3], refs[-3:]
    wide = rhs_ref.shape[1] // len(outs)
    first = pltpu.make_async_copy(inv_hbm, inv_ref, sems.at[0])
    second = pltpu.make_async_copy(rhs_hbm, rhs_ref, sems.at[1])
    first.start()
    second.start()
    first.wait()
    second.wait()
    own, width, _ = inv_ref.shape
    for i, out in enumerate(outs):
        for j in range(own):
            rows = slice(j * width, (j + 1) * width)
            out[rows, :] = jnp.dot(
                inv_ref[j], rhs_ref[rows, i * wide : (i + 1) * wide], preferred_element_type=F32
            ).astype(BF)


def solve_fwd(inv, rhs):
    return pl.pallas_call(
        fwd_kernel,
        in_specs=[pl.BlockSpec(memory_space=pltpu.HBM)] * 2,
        out_shape=[jax.ShapeDtypeStruct((rhs.shape[0], rhs.shape[1] // len(FLIPS)), BF)] * len(FLIPS),
        scratch_shapes=[pltpu.VMEM(inv.shape, BF), pltpu.VMEM(rhs.shape, BF), pltpu.SemaphoreType.DMA((2,))],
        compiler_params=params(63.75),
        name="fwd_low",
    )(inv, rhs)


def sum_kernel(lower, rows, tops, own, ids_ref, tgt_ref, blk_hbm, out_ref, acc_ref, blk_ref, sems):
    steps, per, count, width, _ = blk_ref.shape
    copies = [
        pltpu.make_async_copy(blk_hbm.at[pl.ds(i * per, per)], blk_ref.at[i], sems.at[i]) for i in range(steps)
    ]
    for copy in copies:
        copy.start()
    me_row, me_col = ids_ref[0], ids_ref[1]
    other = (me_row & 1) == 1
    acc_ref[...] = jnp.zeros(acc_ref.shape, F32)
    for i in range(steps):
        copies[i].wait()
        for e in range(per):
            for m in range(count):
                rel = tgt_ref[m, i * per + e] ^ me_col
                low, high = rel & 3, rel >> 2
                low = jnp.where(other & ((low == 1) | (low == 2)), 3 - low, low)
                rel_row = (m // own) ^ me_row
                blk = blk_ref[i, e, m].astype(F32)
                if lower:
                    at = pl.multiple_of(place_of(low, high, tops) * width, width)
                    lanes = slice((m % own) * width, (m % own + 1) * width)
                    acc_ref[rel_row, pl.ds(at, width), lanes] += blk
                else:
                    at = ((((3 - rel_row) & 3) * (rows // 4) + (rel_row >> 2)) * own + m % own) * width
                    acc_ref[4 * high + low, pl.ds(pl.multiple_of(at, width), width), :] += blk
    for i in range(out_ref.shape[0]):
        out_ref[i] = acc_ref[i].astype(BF)


def sum_blocks(lower, ids, targets, blocks, rows, tops, own):
    slots, count, width, _ = blocks.shape
    steps = 4
    shape = (rows, tops * width, own * width) if lower else (tops, rows * own * width, width)
    return pl.pallas_call(
        functools.partial(sum_kernel, lower, rows, tops, own),
        in_specs=[
            pl.BlockSpec(memory_space=pltpu.SMEM),
            pl.BlockSpec(memory_space=pltpu.SMEM),
            pl.BlockSpec(memory_space=pltpu.HBM),
        ],
        out_shape=jax.ShapeDtypeStruct(shape, BF),
        scratch_shapes=[
            pltpu.VMEM(shape, F32),
            pltpu.VMEM((steps, slots // steps, count, width, width), BF),
            pltpu.SemaphoreType.DMA((steps,)),
        ],
        compiler_params=params(48),
        name="sum_lower" if lower else "sum_upper",
    )(ids, targets, blocks)


def pick_kernel(apart, ids_ref, rhs_hbm, low_hbm, up_hbm, rhs_ref, low_ref, up_ref, sems):
    width = low_ref.shape[1]
    copies = []
    for k in range(2):
        at = ids_ref[1] ^ (k * apart)
        for n, (src, dst) in enumerate(
            [
                (rhs_hbm.at[pl.ds(pl.multiple_of(at * width, width), width)], rhs_ref.at[pl.ds(k * width, width)]),
                (low_hbm.at[at], low_ref.at[k]),
                (up_hbm.at[at], up_ref.at[k]),
            ]
        ):
            copies.append(pltpu.make_async_copy(src, dst, sems.at[3 * k + n]))
    for copy in copies:
        copy.start()
    for copy in copies:
        copy.wait()


def pick_top(ids, rhs_top, inv_low, inv_up, apart):
    _, width, _ = inv_low.shape
    return pl.pallas_call(
        functools.partial(pick_kernel, apart),
        in_specs=[pl.BlockSpec(memory_space=pltpu.SMEM)] + [pl.BlockSpec(memory_space=pltpu.HBM)] * 3,
        out_shape=[
            jax.ShapeDtypeStruct((2 * width, rhs_top.shape[1]), BF),
            jax.ShapeDtypeStruct((2, width, width), BF),
            jax.ShapeDtypeStruct((2, width, width), BF),
        ],
        scratch_shapes=[pltpu.SemaphoreType.DMA((6,))],
        compiler_params=params(8),
        name="pick_top",
    )(ids, rhs_top, inv_low, inv_up)


def lower_kernel(begin, mat_ref, p0, p1, p2, p3, *outs):
    pieces = (p0, p1, p2, p3)
    per = outs[0].shape[0]
    deep = mat_ref.shape[2]
    for i, out in enumerate(outs, begin):
        total = None
        for s in range(mat_ref.shape[0]):
            part = jnp.dot(
                mat_ref[s, i * per : (i + 1) * per, :],
                pieces[s % 4][(s // 4) * deep : (s // 4 + 1) * deep, :],
                preferred_element_type=F32,
            )
            total = part if total is None else total + part
        out[...] = total.astype(BF)


def upper_kernel(begin, mat_ref, p0, p1, p2, p3, *outs):
    pieces = (p0, p1, p2, p3)
    per = outs[0].shape[0]
    groups = mat_ref.shape[0] // 4
    for i, out in enumerate(outs, begin):
        total = None
        for g in range(4):
            left = jnp.concatenate(
                [mat_ref[g + 4 * h, i * per : (i + 1) * per, :] for h in range(groups)], axis=1
            )
            part = jnp.dot(left, pieces[g][...], preferred_element_type=F32)
            total = part if total is None else total + part
        out[...] = total.astype(BF)


def apply(kernel, mat, pieces, begin, end, name):
    rows, cols = mat.shape[1], pieces[0].shape[1]
    return pl.pallas_call(
        functools.partial(kernel, begin),
        out_shape=[jax.ShapeDtypeStruct((rows // 4, cols), BF)] * (end - begin),
        compiler_params=params(32 if mat.size * 2 > 4 * MIB else 10),
        name=name,
    )(mat, *pieces)


def top_kernel(rhs_ref, low_ref, up_ref, mine_ref, got_ref, out_ref):
    width = low_ref.shape[1]
    for k in range(2):
        rows, cross = slice(k * width, (k + 1) * width), slice((1 - k) * width, (2 - k) * width)
        lsum = mine_ref[rows, :].astype(F32) + got_ref[cross, :].astype(F32)
        resid = (rhs_ref[rows, :].astype(F32) - lsum).astype(BF)
        fwd = jnp.dot(low_ref[k], resid, preferred_element_type=F32).astype(BF)
        out_ref[rows, :] = jnp.dot(up_ref[k], fwd, preferred_element_type=F32).astype(BF)


def solve_top(picked, mine, got, chunk):
    rhs, inv_low, inv_up = picked
    rows, cols = mine.shape
    return pl.pallas_call(
        top_kernel,
        grid=(1,),
        in_specs=[
            pl.BlockSpec((rows, cols), lambda i: (0, chunk)),
            pl.BlockSpec(inv_low.shape, lambda i: (0, 0, 0)),
            pl.BlockSpec(inv_up.shape, lambda i: (0, 0, 0)),
            pl.BlockSpec((rows, cols), lambda i: (0, 0)),
            pl.BlockSpec((rows, cols), lambda i: (0, 0)),
        ],
        out_specs=pl.BlockSpec((rows, cols), lambda i: (0, 0)),
        out_shape=jax.ShapeDtypeStruct((rows, cols), BF),
        compiler_params=params(8),
        name="solve_top",
    )(rhs, inv_low, inv_up, mine, got)


def low_kernel(parts, inv_ref, fwd_ref, *refs):
    terms, out = refs[:parts], refs[-1]
    own, width, _ = inv_ref.shape
    for j in range(own):
        rows = slice(j * width, (j + 1) * width)
        usum = terms[0][rows, :].astype(F32)
        for term in terms[1:]:
            usum = usum + term[rows, :].astype(F32)
        resid = (fwd_ref[rows, :].astype(F32) - usum).astype(BF)
        out[rows, :] = jnp.dot(inv_ref[j], resid, preferred_element_type=F32).astype(BF)


def solve_low(inv, fwd, terms, into, chunk, chunks):
    rows, cols = fwd.shape
    more = [] if into is None else [into]
    return pl.pallas_call(
        functools.partial(low_kernel, len(terms)),
        grid=(1,),
        in_specs=[
            pl.BlockSpec(inv.shape, lambda i: (0, 0, 0)),
            pl.BlockSpec((rows, cols), lambda i: (0, 0)),
        ]
        + [pl.BlockSpec((rows, cols), lambda i: (0, 0))] * len(terms)
        + [pl.BlockSpec(memory_space=pl.ANY)] * len(more),
        out_specs=pl.BlockSpec((rows, cols), lambda i: (0, chunk)),
        out_shape=jax.ShapeDtypeStruct((rows, cols * chunks), BF),
        input_output_aliases={2 + len(terms): 0} if more else {},
        compiler_params=params(8),
        name="solve_low",
    )(inv, fwd, *terms, *more)


def swap(x, axis, bit):
    size = lax.axis_size(axis)
    return lax.ppermute(x, axis, [(i, i ^ (1 << bit)) for i in range(size)])


def cross(x, bit, flip):
    rows, cols = lax.axis_size("row"), lax.axis_size("col")
    pairs = [(r * cols + c, r * cols + (c ^ (1 << (bit ^ flip ^ (r & 1))))) for r in range(rows) for c in range(cols)]
    return lax.ppermute(x, ("row", "col"), pairs)


def add(*xs):
    total = xs[0].astype(F32)
    for x in xs[1:]:
        total = total + x.astype(F32)
    return total.astype(BF)


def weave(x, y, size):
    w = x.shape[1]
    return jnp.concatenate([x.reshape(-1, 1, size, w), y.reshape(-1, 1, size, w)], axis=1).reshape(-1, w)


def odd(x, size):
    return x.reshape(-1, 2, size, x.shape[1])[:, 1].reshape(-1, x.shape[1])


def even(x, size):
    return x.reshape(-1, 2, size, x.shape[1])[:, 0].reshape(-1, x.shape[1])


def after(x, *done):
    return lax.optimization_barrier((x, *done))[0]


def far_row(own):
    held = own
    for bit in reversed(range(2, lax.axis_size("row").bit_length() - 1)):
        held = weave(held, swap(held, "row", bit), own.shape[0])
    return held, swap(held, "row", 1)


def sums_col(terms, size):
    for bit in range(2, lax.axis_size("col").bit_length() - 2):
        new = swap(add(*[odd(t, size) for t in terms]), "col", bit)
        terms = [even(t, size) for t in terms] + [new]
    return add(*terms)


def widen_col(held, size):
    for bit in reversed(range(2, lax.axis_size("col").bit_length() - 2)):
        held = weave(held, swap(held, "col", bit), size)
    return held


def sums_row(terms, size):
    for bit in range(2, lax.axis_size("row").bit_length() - 1):
        new = swap(add(*[odd(t, size) for t in terms]), "row", bit)
        terms = [even(t, size) for t in terms] + [new]
    return terms


def body(
    rhs_low,
    rhs_top,
    lower_blocks,
    upper_blocks,
    block_target,
    inv_lower_low,
    inv_upper_low,
    inv_lower_top,
    inv_upper_top,
):
    own, width, _ = inv_lower_low.shape
    rows, cols = lax.axis_size("row"), lax.axis_size("col")
    tops = inv_lower_top.shape[0]
    assert tops == cols and rows >= 4 and cols >= 8
    last = cols.bit_length() - 2
    ids = jnp.stack([lax.axis_index("row"), lax.axis_index("col")]).astype(jnp.int32)
    targets = block_target.T

    fwds = solve_fwd(inv_lower_low, rhs_low)
    near, far = zip(*[far_row(fwd) for fwd in fwds])
    side = [swap(x, "row", 0) for x in near]
    mat_l = sum_blocks(True, ids, targets, lower_blocks, rows, tops, own)
    far_side = [swap(after(x, mat_l), "row", 0) for x in far]
    pieces = list(zip(near, side, far, far_side))
    parts = [apply(lower_kernel, mat_l, p, 0, 1, "first_lower") for p in pieces]
    parts = [x + apply(lower_kernel, mat_l, p, 1, 4, "apply_lower") for x, p in zip(parts, pieces)]
    mine = []
    for i, (three, one, two, zero) in enumerate(parts):
        flip = FLIPS[i]
        if flip:
            one, two = two, one
        got = cross(three, 0, flip)
        rest = cross(one, 0, flip)
        more = cross(add(two, got), 1, flip)
        mine.append(sums_col([zero, rest, more], width))
    other = [swap(x, "col", last) for x in mine]
    mat_u = sum_blocks(False, after(ids, mine[-1]), targets, upper_blocks, rows, tops, own)
    picked = pick_top(after(ids, mat_u), rhs_top, inv_lower_top, inv_upper_top, cols // 2)
    sol_low = None
    top_parts, solved = [], []
    for i, flip in enumerate(FLIPS):
        both = solve_top(picked, mine[i], other[i], i)
        top_parts.append(both[:width])
        zero = widen_col(both, width)
        two = cross(zero, 1, flip)
        one = cross(zero, 0, flip)
        three = cross(after(two, one), 0, flip)
        if flip:
            one, two = two, one
        solved.append((zero, one, two, three))
    begun, sent = [], []
    for pieces in solved:
        three, two = apply(upper_kernel, mat_u, pieces, 0, 2, "first_upper")
        send = add(two, after(swap(three, "row", 0), *begun))
        sent.append(send)
        begun.append(swap(send, "row", 1).astype(F32))
    for i, pieces in enumerate(solved):
        pieces = (after(pieces[0], *sent[: i + 1]), *pieces[1:])
        one, zero = apply(upper_kernel, mat_u, pieces, 2, 4, "apply_upper")
        part = zero.astype(F32) + begun[i]
        terms = sums_row([part, swap(one, "row", 0)], own * width)
        sol_low = solve_low(inv_upper_low, fwds[i], terms, sol_low, i, len(FLIPS))
    top_parts[0] = after(top_parts[0], *sent)
    return sol_low, jnp.concatenate(top_parts, axis=1)


def solution(mesh):
    placed = (
        P(("row", "col"), None),
        P("row", None),
        P("row", "col", None, None),
        P("row", "col", None, None),
        P("row", "col"),
        P(("row", "col"), None, None),
        P(("row", "col"), None, None),
        P("row", None, None),
        P("row", None, None),
    )
    return jax.shard_map(
        body,
        mesh=mesh,
        in_specs=placed,
        out_specs=(P(("row", "col"), None), P(("row", "col"), None)),
        check_vma=False,
    )
```
